256 devices in a mesh: harm: 32 (over y_lo, z, core), band: 8 (over y_hi, x).
Axes of the slice: x: 4, y: 4 (y_hi: 2, y_lo: 2; y = y_hi * 2 + y_lo), z: 8, core: 2. Of those that a mesh axis runs over, the one named last changes fastest.
Arguments:
- right_side: float32 [64, 4, 5120], P('harm'), may hold values from -50 to 50
- inv_spectra: float32 [2, 5120], replicated, may hold values from 0.1 to 10
- beam: float32 [5120], replicated, may hold values from 0.2 to 1
- m_values: int32 [64], P('harm'), may hold values from 0 to 5119, as said below
- legendre: bfloat16 [64, 2, 5120, 1024], P('harm', None, None, 'band'), may hold values from -0.078125 to 0.078125
- stencil_weights: float32 [16, 32, 8, 32, 128], P(None, 'harm', 'band'), may hold values from -0.25 to 0.5
- stencil_base: int32 [2, 32, 8, 32, 128], P(None, 'harm', 'band'), may hold values from 0 to 640, as said below
- inv_noise: float32 [2, 32, 8, 32, 128], P(None, 'harm', 'band'), may hold values from 0.25 to 4
- slot_counts: int32 [32, 8, 32], P('harm', 'band'), may hold values from 16 to 128, as said below
Outputs:
- solution_coefs: float32 [64, 4, 5120], P('harm', None, 'band')
- residual: float32 [64, 4, 5120], P('harm', None, 'band')
The draws below stay inside these ranges and needn't reach their ends.
Inputs may be any that keep to these rules, and one draw needn't show every extreme that they name: `m_values`: distinct values. `stencil_base`: row 0 lies in 0 .. 128, row 1 in 0 .. 640. `slot_counts`: in every band some pixel owner receives 128 live slots from every device of the band.
All inputs are finite; a program needn't handle non-finite values.
Results may differ from the reference program's by a relative error of at most 0.0039.
Values may be sent and summed in bfloat16 or wider, within the bound.
No kernel may reach another device: no remote copies, remote signals or barrier semaphores. Data moves between devices by JAX's collectives and lax.ppermute only.
A program may use at most 64 MiB of HBM per device.

```python
import math
import jax
import jax.numpy as jnp
from jax import lax

LMAX = 5120
NPHI = 20480
R_DEV = 128
CAP = 128
M_TOT = 64
CYCLES = 1024
PHI_DEV = 640
N_HARM = 32
N_BAND = 8


def draw_right_side(key, part):
    key = jax.random.fold_in(key, 11)
    key_base = jax.random.fold_in(key, 1)
    key_rows = jax.random.fold_in(key, 2)
    key_cols = jax.random.fold_in(key, 3)
    full_shape = (M_TOT, 4, LMAX)
    ramp_scale = jnp.sqrt(1.0 + 2.0 * jnp.arange(M_TOT, dtype=jnp.float32) / max(M_TOT - 1, 1))
    base_draw = jnp.clip(jax.random.normal(key_base, full_shape, jnp.float32), -4.0, 4.0)
    row_scale = 10.0 ** (jax.random.uniform(key_rows, (M_TOT, 4, 1), jnp.float32) - 0.5)
    col_scale = 10.0 ** (0.5 * jax.random.uniform(key_cols, (1, 1, LMAX), jnp.float32) - 0.25)
    return (base_draw * row_scale * col_scale * ramp_scale[:, None, None]).astype(jnp.float32)


def draw_m_values(key, part):
    key = jax.random.fold_in(key, 23)
    key_pick = jax.random.fold_in(key, 1)
    key_order = jax.random.fold_in(key, 2)
    middle = jax.random.permutation(key_pick, LMAX - 2)[:M_TOT - 2].astype(jnp.int32) + 1
    chosen = jnp.concatenate([jnp.array([0, LMAX - 1], jnp.int32), middle])
    return chosen[jax.random.permutation(key_order, M_TOT)].astype(jnp.int32)


def draw_stencil_base(key, part):
    key = jax.random.fold_in(key, 37)
    key_rows = jax.random.fold_in(key, 1)
    key_cols = jax.random.fold_in(key, 2)
    full_shape = (N_HARM, N_BAND, N_HARM, CAP)
    first_rows = jax.random.randint(key_rows, full_shape, 0, R_DEV + 1, jnp.int32)
    first_cols = jax.random.randint(key_cols, full_shape, 0, PHI_DEV + 1, jnp.int32)
    first_rows = first_rows.at[0, 0, 0, 0].set(R_DEV).at[0, 0, 0, 1].set(0)
    first_cols = first_cols.at[0, 0, 0, 0].set(PHI_DEV).at[0, 0, 0, 1].set(0)
    return jnp.stack([first_rows, first_cols]).astype(jnp.int32)


def draw_slot_counts(key, part):
    key = jax.random.fold_in(key, 41)
    key_level = jax.random.fold_in(key, 1)
    key_owner = jax.random.fold_in(key, 2)
    full_shape = (N_HARM, N_BAND, N_HARM)
    halving = jax.random.randint(key_level, full_shape, 0, 4, jnp.int32)
    counts = CAP // jnp.power(2, halving).astype(jnp.int32)
    busy_owner = jax.random.randint(key_owner, (1, N_BAND, 1), 0, N_HARM, jnp.int32)
    owner_mask = lax.broadcasted_iota(jnp.int32, full_shape, 2) == busy_owner
    return jnp.where(owner_mask, CAP, counts).astype(jnp.int32)


def levels(own_key, shape, cuts, low, largest):
    factor_of = 1.0
    for position, shards_of in cuts:
        heights = jax.random.uniform(jax.random.fold_in(jax.random.fold_in(own_key, 6), position), (shards_of,), jnp.float32, low / len(cuts), largest / len(cuts))
        factor_of = factor_of * jnp.repeat(jnp.exp(heights), shape[position] // shards_of).reshape((-1,) + (1,) * (len(shape) - 1 - position))
    return factor_of


def normal_values(stream_key, extent, width, limit, pieces=(), kind=jnp.bfloat16):
    loudness = levels(stream_key, extent, pieces, -0.22, 0.18) if pieces else 1.0
    values = jax.random.normal(stream_key, extent, jnp.float32) * width * loudness
    return jnp.minimum(jnp.maximum(values, -limit), limit).astype(kind)


def setup_inputs(seed: int = 0) -> dict:
    key_of = jax.random.split(jax.random.key(seed), 10)
    right_side = draw_right_side(jax.random.fold_in(key_of[9], 71), 0)
    inv_spectra = jnp.clip(jnp.exp(jax.random.uniform(key_of[1], (2, LMAX), jnp.float32, math.log(0.1), math.log(10.0))), 0.1, 10.0)
    beam = jnp.clip(jnp.exp(jax.random.uniform(key_of[2], (LMAX,), jnp.float32, math.log(0.2), math.log(1.0))), 0.2, 1.0)
    m_values = draw_m_values(jax.random.fold_in(key_of[9], 71), 0)
    legendre = normal_values(key_of[4], (M_TOT, 2, LMAX, CYCLES), LMAX ** -0.5, 0.078125, ((0, 32), (3, 8)))
    stencil_weights = jnp.clip(-0.25 + 0.75 * jax.random.uniform(key_of[5], (16, N_HARM, N_BAND, N_HARM, CAP), jnp.float32) ** levels(key_of[5], (16, N_HARM, N_BAND, N_HARM, CAP), ((1, 32), (2, 8)), -0.2, 0.2), -0.25, 0.5)
    stencil_base = draw_stencil_base(jax.random.fold_in(key_of[9], 71), 0)
    inv_noise = jnp.clip(jnp.exp(math.log(4.0) - 2.7725887 * jax.random.uniform(key_of[7], (2, N_HARM, N_BAND, N_HARM, CAP), jnp.float32) ** levels(key_of[7], (2, N_HARM, N_BAND, N_HARM, CAP), ((1, 32), (2, 8)), -0.2, 0.2)), 0.25, 4.0)
    slot_counts = draw_slot_counts(jax.random.fold_in(key_of[9], 71), 0)
    return {"right_side": right_side, "inv_spectra": inv_spectra, "beam": beam, "m_values": m_values, "legendre": legendre, "stencil_weights": stencil_weights, "stencil_base": stencil_base, "inv_noise": inv_noise, "slot_counts": slot_counts}


def spin_fields(cycle_modes):
    q_real = -(cycle_modes[:, 0, 0] - cycle_modes[:, 3, 1])
    q_imag = -(cycle_modes[:, 1, 0] + cycle_modes[:, 2, 1])
    u_real = -(cycle_modes[:, 2, 0] + cycle_modes[:, 1, 1])
    u_imag = -(cycle_modes[:, 3, 0] - cycle_modes[:, 0, 1])
    return jnp.stack([q_real, q_imag, u_real, u_imag], axis=1)


def spin_adjoint(fields):
    q_real = fields[:, 0]
    q_imag = fields[:, 1]
    u_real = fields[:, 2]
    u_imag = fields[:, 3]
    plus_part = jnp.stack([-q_real, -q_imag, -u_real, -u_imag], axis=1)
    minus_part = jnp.stack([u_imag, -u_real, -q_imag, q_real], axis=1)
    return jnp.stack([plus_part, minus_part], axis=2)


def phase_tables(modes_list, pixels, cycle_length, total_modes):
    turn_count = (modes_list[:, None] * pixels) % cycle_length
    angles = turn_count.astype(jnp.float32) * (2.0 * math.pi / cycle_length)
    weight = jnp.where(modes_list == 0, 1.0, 2.0).astype(jnp.float32) * (2.0 * total_modes) ** -0.5
    return weight[:, None] * jnp.cos(angles), weight[:, None] * jnp.sin(angles)


def reference(right_side, inv_spectra, beam, m_values, legendre, stencil_weights, stencil_base, inv_noise, slot_counts):
    coef_in = (right_side * beam[None, None, :]).astype(jnp.bfloat16)

    def synth_one(pair_in):
        coef_row, table_m = pair_in
        return jnp.einsum("cl,tlr->ctr", coef_row.astype(jnp.float32), table_m.astype(jnp.float32))

    cycle_modes = lax.map(synth_one, (coef_in, legendre))
    fields = spin_fields(cycle_modes)
    pixels = lax.broadcasted_iota(jnp.int32, (1, NPHI), 1)
    cos_tab, sin_tab = phase_tables(m_values, pixels, NPHI, M_TOT)
    phase_table = jnp.concatenate([cos_tab, -sin_tab], axis=0)
    stacked = jnp.concatenate([fields[:, 0::2], fields[:, 1::2]], axis=0)
    sky_map = jnp.einsum("mfr,mj->frj", stacked, phase_table, precision=lax.Precision.HIGHEST)
    sky_map = sky_map.astype(jnp.bfloat16)
    padded = jnp.concatenate([sky_map[:, :, -2:], sky_map, sky_map[:, :, :2]], axis=2)
    padded = jnp.pad(padded, ((0, 0), (2, 2), (0, 0)))
    row_width = NPHI + 4
    flat_sky = padded.reshape(2, -1)
    entries = jnp.arange(16, dtype=jnp.int32)
    tile_row = entries // 4
    tile_col = entries % 4
    harm_ids = lax.broadcasted_iota(jnp.int32, (N_HARM, N_HARM, CAP), 1)
    slot_ids = lax.broadcasted_iota(jnp.int32, (N_HARM, N_HARM, CAP), 2)

    def band_step(accum, band_id):
        weights = lax.dynamic_index_in_dim(stencil_weights, band_id, 2, keepdims=False)
        noise_gain = lax.dynamic_index_in_dim(inv_noise, band_id, 2, keepdims=False)
        tile_base = lax.dynamic_index_in_dim(stencil_base, band_id, 2, keepdims=False)
        counts = lax.dynamic_index_in_dim(slot_counts, band_id, 1, keepdims=False)
        alive_slots = slot_ids < counts[:, :, None]
        weights = jnp.where(alive_slots[None], weights, 0.0)
        noise_gain = jnp.where(alive_slots[None], noise_gain, 0.0)
        first_row = band_id * R_DEV + tile_base[0]
        first_col = harm_ids * PHI_DEV + tile_base[1]
        tile_index = (first_row[None] + tile_row[:, None, None, None]) * row_width + first_col[None] + tile_col[:, None, None, None]
        values = flat_sky[:, tile_index].astype(jnp.float32)
        sampled = jnp.sum(weights[None] * values, axis=1)
        weighted = noise_gain * sampled
        accum = accum.at[:, tile_index.reshape(-1)].add((weights[None] * weighted[:, None]).reshape(2, -1))
        return accum, None

    spread, _ = lax.scan(band_step, jnp.zeros(flat_sky.shape, jnp.float32), jnp.arange(N_BAND, dtype=jnp.int32))
    spread_grid = spread.reshape(padded.shape)[:, 2:-2, :]
    back_sky = spread_grid[:, :, 2:-2]
    back_sky = back_sky.at[:, :, :2].add(spread_grid[:, :, -2:])
    back_sky = back_sky.at[:, :, -2:].add(spread_grid[:, :, :2])
    real_part = jnp.einsum("frj,mj->mfr", back_sky, cos_tab, precision=lax.Precision.HIGHEST)
    imag_part = -jnp.einsum("frj,mj->mfr", back_sky, sin_tab, precision=lax.Precision.HIGHEST)
    back_fields = jnp.stack([real_part, imag_part], axis=2).reshape(M_TOT, 4, CYCLES)
    back_modes = spin_adjoint(back_fields).astype(jnp.bfloat16)

    def analyse_one(pair_in):
        mode_row, table_m = pair_in
        return jnp.einsum("ctr,tlr->cl", mode_row.astype(jnp.float32), table_m.astype(jnp.float32))

    harmonic = lax.map(analyse_one, (back_modes, legendre))
    spectra = jnp.repeat(inv_spectra, 2, axis=0)
    image_vec = spectra[None] * right_side + beam[None, None, :] * harmonic
    norm_sq = jnp.sum(right_side * right_side)
    curvature = jnp.sum(right_side * image_vec)
    step_size = norm_sq / curvature
    return step_size * right_side, right_side - step_size * image_vec
```

```python
import functools
import math

import jax
import jax.numpy as jnp
from jax import lax
from jax.experimental import pallas as pl
from jax.experimental.pallas import tpu as pltpu
from jax.sharding import PartitionSpec as P

NPHI = 20480
ROWS = 144
LANES = 256
BLOCK = 256
F32 = jnp.float32
BF16 = jnp.bfloat16


def split3(value):
    first = value.astype(BF16).astype(F32)
    rest = value - first
    second = rest.astype(BF16).astype(F32)
    third = (rest - second).astype(BF16).astype(F32)
    return first, second, third


def trig_tables(modes):
    lane = lax.broadcasted_iota(jnp.int32, (64, 128), 1)
    digit = lane & 31
    steps = jnp.where(
        lane < 32, digit * 1024, jnp.where(lane < 64, digit * 32, jnp.where(lane < 96, digit, lane & 3))
    )
    product = modes * steps
    high = product >> 12
    turn = (high - 5 * ((high * 52429) >> 18)) * 4096 + (product & 4095)
    quarter = jnp.zeros_like(turn)
    for edge in (2560, 7680, 12800, 17920):
        quarter = quarter + (turn >= edge).astype(jnp.int32)
    angle = (turn - 5120 * quarter).astype(F32) * (2.0 * math.pi / NPHI)
    quarter = quarter & 3
    sq = angle * angle
    sine = angle * (1.0 + sq * (-1.0 / 6 + sq * (1.0 / 120 + sq * (-1.0 / 5040 + sq * (1.0 / 362880)))))
    cosine = 1.0 + sq * (
        -0.5 + sq * (1.0 / 24 + sq * (-1.0 / 720 + sq * (1.0 / 40320 - sq * (1.0 / 3628800))))
    )
    cos_out = jnp.where(
        quarter == 0, cosine, jnp.where(quarter == 1, -sine, jnp.where(quarter == 2, -cosine, sine))
    )
    sin_out = jnp.where(
        quarter == 0, sine, jnp.where(quarter == 1, cosine, jnp.where(quarter == 2, -sine, -cosine))
    )
    return cos_out, sin_out


def points_kernel(blocks_ref, sums_ref, x_ref, data_ref, out_ref, table_ref, field_ref, acc_ref, curv_ref):
    row_id = lax.broadcasted_iota(jnp.int32, (256, 256), 0)
    col_id = lax.broadcasted_iota(jnp.int32, (256, 256), 1)
    to_mode_last = (col_id == 4 * (row_id & 63) + (row_id >> 6)).astype(F32).astype(BF16)
    to_mode_first = (row_id == 4 * (col_id & 63) + (col_id >> 6)).astype(F32).astype(BF16)
    fields = jnp.dot(to_mode_last, x_ref[...], preferred_element_type=F32)
    field_ref[...] = fields.astype(BF16)
    head = fields[:64]
    head_lane = lax.broadcasted_iota(jnp.int32, (64, LANES), 1)
    mode_value = jnp.sum(
        jnp.where(head_lane == 132, head * 64.0, jnp.where(head_lane == 133, head, 0.0)),
        axis=1,
        keepdims=True,
    )
    modes = jnp.broadcast_to(mode_value, (64, 128)).astype(jnp.int32)
    cos_tab, sin_tab = trig_tables(modes)
    weight = jnp.where(modes == 0, 1.0, 2.0).astype(F32) * 128.0**-0.5
    lane = lax.broadcasted_iota(jnp.int32, (64, 128), 1)
    groups = [
        (lane < 32, weight),
        ((lane >= 32) & (lane < 64), None),
        ((lane >= 64) & (lane < 96), None),
    ]
    for a in range(4):
        groups.append(((lane >= 96) & (((lane - 96) & 15) >> 2 == a), None))
    for index, (mask, gain) in enumerate(groups):
        for part, table in enumerate((cos_tab, sin_tab)):
            value = table if gain is None else table * gain
            value = jnp.where(mask, value, 0.0)
            rounded = value.astype(BF16)
            start = (2 * index + part) * 64
            table_ref[pl.ds(start, 64), 0:128] = rounded
            table_ref[pl.ds(start, 64), 128:256] = (value - rounded.astype(F32)).astype(BF16)
    acc_ref[...] = jnp.zeros_like(acc_ref)
    curv_ref[...] = jnp.zeros_like(curv_ref)

    def block_step(index, carry):
        data = data_ref[:, pl.ds(pl.multiple_of(index * BLOCK, BLOCK), BLOCK)]
        pixel = data[17:18].astype(jnp.int32)
        first_row = data[16:17].astype(jnp.int32)
        digit_id = lax.broadcasted_iota(jnp.int32, (96, BLOCK), 0)
        hit = (
            (digit_id == (pixel >> 10))
            | (digit_id == ((pixel >> 5) & 31) + 32)
            | (digit_id == (pixel & 31) + 64)
        )
        weights = data[0:16]
        weights_high = weights.astype(BF16)
        weights_low = (weights - weights_high.astype(F32)).astype(BF16)
        chosen = jnp.concatenate([hit.astype(F32).astype(BF16), weights_high, weights_low], axis=0)
        phases = jnp.dot(
            table_ref[...], jnp.concatenate([chosen, chosen], axis=0), preferred_element_type=F32
        )
        part = [phases[64 * i : 64 * (i + 1)] for i in range(14)]
        mid_re = part[0] * part[2] - part[1] * part[3]
        mid_im = part[0] * part[3] + part[1] * part[2]
        turn_re = mid_re * part[4] - mid_im * part[5]
        turn_im = mid_re * part[5] + mid_im * part[4]
        grid_row = lax.broadcasted_iota(jnp.int32, (ROWS, BLOCK), 0)
        total = [jnp.zeros((64, BLOCK), F32), jnp.zeros((64, BLOCK), F32)]
        hits = []
        waves = []
        for a in range(4):
            wave_re = turn_re * part[6 + 2 * a] - turn_im * part[7 + 2 * a]
            wave_im = turn_re * part[7 + 2 * a] + turn_im * part[6 + 2 * a]
            row_hit = (grid_row == first_row + a).astype(F32).astype(BF16)
            picked = jnp.dot(field_ref[:, 0:ROWS], row_hit, preferred_element_type=F32)
            for f in range(2):
                total[f] = (
                    total[f]
                    + picked[128 * f : 128 * f + 64] * wave_re
                    - picked[128 * f + 64 : 128 * f + 128] * wave_im
                )
            hits.append(row_hit)
            waves.append((wave_re, wave_im))
        weighted = []
        for f in range(2):
            sampled = jnp.sum(total[f], axis=0, keepdims=True)
            value = data[18 + f : 19 + f] * sampled
            curv_ref[f : f + 1, :] += value * sampled
            weighted.append(value)
        update = jnp.zeros((256, ROWS), F32)
        for a in range(4):
            wave_re, wave_im = waves[a]
            terms = jnp.concatenate(
                [
                    weighted[0] * wave_re,
                    -(weighted[0] * wave_im),
                    weighted[1] * wave_re,
                    -(weighted[1] * wave_im),
                ],
                axis=0,
            ).astype(BF16)
            update = update + lax.dot_general(
                terms, hits[a], (((1,), (1,)), ((), ())), preferred_element_type=F32
            )
        acc_ref[:, 0:ROWS] += update
        return carry

    lax.fori_loop(0, blocks_ref[0], block_step, 0)
    back = jnp.dot(to_mode_first, acc_ref[...].astype(BF16), preferred_element_type=F32)
    curvature = jnp.sum(curv_ref[...], axis=(0, 1), keepdims=True) + sums_ref[1]
    norm = jnp.zeros((1, 1), F32) + sums_ref[0]
    for offset, piece in enumerate(split3(curvature) + split3(norm)):
        back = jnp.where(col_id == 132 + offset, piece, back)
    out_ref[...] = back.astype(BF16)


def analysis_kernel(got_ref, legendre_ref, edge_ref, out_ref, own_ref, rim_ref, sums_ref):
    @pl.when(pl.program_id(0) == 0)
    def _():
        total = got_ref[0].astype(F32)
        for source in range(1, 32):
            total = total + got_ref[source].astype(F32)
        lane = lax.broadcasted_iota(jnp.int32, (8, 128), 1)
        row = lax.broadcasted_iota(jnp.int32, (8, 128), 0)
        low, high = total[:, 0:128], total[:, 128:256]
        curvature = jnp.sum(jnp.where((lane >= 4) & (lane < 7), high, 0.0), axis=1, keepdims=True)
        norm = jnp.sum(jnp.where((lane >= 7) & (lane < 10), high, 0.0), axis=1, keepdims=True)
        sums_ref[...] = jnp.where(lane == 0, curvature, jnp.where(lane == 1, norm, 0.0))
        own = pltpu.roll(total, 254, 1)[:, 0:128]
        rim = jnp.where(lane < 2, low, jnp.where(lane < 4, high, 0.0))
        for ref, value in ((own_ref, own), (rim_ref, rim)):
            plus = -value
            minus = jnp.concatenate(
                [
                    value[3:4],
                    -value[2:3],
                    -value[1:2],
                    value[0:1],
                    value[7:8],
                    -value[6:7],
                    -value[5:6],
                    value[4:5],
                ],
                axis=0,
            )
            for m in range(2):
                keep = (row >> 2) == m
                ref[2 * m] = jnp.where(keep, plus, 0.0).astype(BF16)
                ref[2 * m + 1] = jnp.where(keep, minus, 0.0).astype(BF16)

    chunk = legendre_ref.shape[2]
    result = jnp.zeros((8, chunk), F32)
    for m in range(2):
        for t in range(2):
            result = result + lax.dot_general(
                own_ref[2 * m + t],
                legendre_ref[m, t],
                (((1,), (1,)), ((), ())),
                preferred_element_type=F32,
            )
            result = result + jnp.dot(
                rim_ref[2 * m + t][:, 0:16], edge_ref[m, t], preferred_element_type=F32
            )
    out_ref[0, :, 0:chunk] = result
    out_ref[0, :, chunk : chunk + 128] = sums_ref[...]


def spin_fields(cycle_modes):
    q_real = -(cycle_modes[:, 0, 0] - cycle_modes[:, 3, 1])
    q_imag = -(cycle_modes[:, 1, 0] + cycle_modes[:, 2, 1])
    u_real = -(cycle_modes[:, 2, 0] + cycle_modes[:, 1, 1])
    u_imag = -(cycle_modes[:, 3, 0] - cycle_modes[:, 0, 1])
    return jnp.stack([q_real, q_imag, u_real, u_imag], axis=1)


def local(
    right_side,
    inv_spectra,
    beam,
    m_values,
    legendre,
    stencil_weights,
    stencil_base,
    inv_noise,
    slot_counts,
):
    band_count = lax.axis_size("band")
    lmax_len = right_side.shape[2]
    share_len = lmax_len // band_count

    pick_row = lax.broadcasted_iota(jnp.int32, (4, 128), 0)
    pick_col = lax.broadcasted_iota(jnp.int32, (4, 128), 1)
    pick = (pick_col == jnp.where(pick_row < 2, pick_row, pick_row + 124)).astype(BF16)
    edges = jnp.einsum("kr,mtlr->mtkl", pick, legendre, preferred_element_type=F32).astype(BF16)
    up = [(i, i + 1) for i in range(band_count - 1)]
    down = [(i + 1, i) for i in range(band_count - 1)]
    low_rim = lax.ppermute(edges[:, :, 2:4], "band", up)
    high_rim = lax.ppermute(edges[:, :, 0:2], "band", down)
    rim = jnp.concatenate([low_rim, high_rim], axis=2)

    coef_in = (right_side * beam[None, None, :]).astype(BF16)
    own_modes = jnp.einsum("mcl,mtlr->mctr", coef_in, legendre, preferred_element_type=F32)
    rim_modes = jnp.einsum("mcl,mtkl->mctk", coef_in, rim, preferred_element_type=F32)
    cycle_modes = jnp.concatenate([rim_modes[..., 0:2], own_modes, rim_modes[..., 2:4]], axis=3)
    fields = spin_fields(cycle_modes)
    mode_parts = jnp.stack([m_values >> 6, m_values & 63], axis=1).astype(F32)
    mode_parts = jnp.broadcast_to(mode_parts[:, None, :], (2, 4, 2))
    sent = jnp.concatenate([fields, mode_parts, jnp.zeros((2, 4, LANES - 134), F32)], axis=2)
    sent = sent.astype(BF16).reshape(1, 8, LANES)
    got = lax.all_to_all(
        jnp.broadcast_to(sent, (32, 8, LANES)), "harm", split_axis=0, concat_axis=0, tiled=True
    )

    slots = stencil_weights.shape[4]
    alive = lax.broadcasted_iota(jnp.int32, (32, slots), 1) < slot_counts.reshape(32, 1)
    weights = jnp.where(alive[None], stencil_weights.reshape(16, 32, slots), 0.0)
    noise = jnp.where(alive[None], inv_noise.reshape(2, 32, slots), 0.0)
    base = stencil_base.reshape(2, 32, slots)
    owner = lax.broadcasted_iota(jnp.int32, (32, slots), 0)
    pixel = owner * 640 + base[1] - 2
    pixel = jnp.where(pixel < 0, pixel + NPHI, jnp.where(pixel >= NPHI, pixel - NPHI, pixel))
    data = jnp.concatenate(
        [
            weights,
            base[0:1].astype(F32),
            pixel[None].astype(F32),
            noise,
            jnp.zeros((4, 32, slots), F32),
        ],
        axis=0,
    ).reshape(24, 32 * slots)

    spectra = jnp.repeat(inv_spectra, 2, axis=0)
    norm_part = jnp.sum(right_side * right_side)
    prior_part = jnp.sum(spectra[None] * right_side * right_side)
    sums = jnp.stack([norm_part, prior_part]) / band_count
    blocks = jnp.full((1,), 32 * slots // BLOCK, jnp.int32)
    back = pl.pallas_call(
        points_kernel,
        out_shape=jax.ShapeDtypeStruct((256, LANES), BF16),
        in_specs=[
            pl.BlockSpec(memory_space=pltpu.SMEM),
            pl.BlockSpec(memory_space=pltpu.SMEM),
            pl.BlockSpec(memory_space=pltpu.VMEM),
            pl.BlockSpec(memory_space=pltpu.VMEM),
        ],
        out_specs=pl.BlockSpec(memory_space=pltpu.VMEM),
        scratch_shapes=[
            pltpu.VMEM((896, 256), BF16),
            pltpu.VMEM((256, LANES), BF16),
            pltpu.VMEM((256, LANES), F32),
            pltpu.VMEM((2, BLOCK), F32),
        ],
        compiler_params=pltpu.CompilerParams(vmem_limit_bytes=32 * 1024 * 1024),
        name="points",
    )(blocks, sums, got.reshape(256, LANES), data)

    back_got = lax.all_to_all(
        back.reshape(32, 8, LANES), "harm", split_axis=0, concat_axis=0, tiled=True
    )
    rim_rows = jnp.concatenate([rim, jnp.zeros((2, 2, 12, lmax_len), BF16)], axis=2)
    harmonic = pl.pallas_call(
        analysis_kernel,
        grid=(band_count,),
        out_shape=jax.ShapeDtypeStruct((band_count, 8, share_len + 128), F32),
        in_specs=[
            pl.BlockSpec((32, 8, LANES), lambda i: (0, 0, 0)),
            pl.BlockSpec((2, 2, share_len, 128), lambda i: (0, 0, i, 0)),
            pl.BlockSpec((2, 2, 16, share_len), lambda i: (0, 0, 0, i)),
        ],
        out_specs=pl.BlockSpec((1, 8, share_len + 128), lambda i: (i, 0, 0)),
        scratch_shapes=[
            pltpu.VMEM((4, 8, 128), BF16),
            pltpu.VMEM((4, 8, 128), BF16),
            pltpu.VMEM((8, 128), F32),
        ],
        compiler_params=pltpu.CompilerParams(vmem_limit_bytes=32 * 1024 * 1024),
        name="analysis",
    )(back_got, legendre, rim_rows)

    parts = lax.all_to_all(harmonic, "band", split_axis=0, concat_axis=0, tiled=True)
    total = jnp.sum(parts, axis=0)
    step_size = total[0, share_len + 1] / total[0, share_len]
    offset = lax.axis_index("band") * share_len
    own_rhs = lax.dynamic_slice_in_dim(right_side, offset, share_len, 2)
    own_spectra = lax.dynamic_slice_in_dim(spectra, offset, share_len, 1)
    own_beam = lax.dynamic_slice_in_dim(beam, offset, share_len, 0)
    own_image = own_spectra[None] * own_rhs + own_beam[None, None] * total[:, 0:share_len].reshape(
        2, 4, share_len
    )
    return (step_size * own_rhs, own_rhs - step_size * own_image)


def solution(mesh):
    placed = (
        P("harm", None, None),
        P(),
        P(),
        P("harm"),
        P("harm", None, None, "band"),
        P(None, "harm", "band", None, None),
        P(None, "harm", "band", None, None),
        P(None, "harm", "band", None, None),
        P("harm", "band", None),
    )
    return jax.shard_map(
        local,
        mesh=mesh,
        in_specs=placed,
        out_specs=(P("harm", None, "band"), P("harm", None, "band")),
        check_vma=False,
    )
```

```python
import functools
import math

import jax
import jax.numpy as jnp
from jax import lax
from jax.experimental import pallas as pl
from jax.experimental.pallas import tpu as pltpu
from jax.sharding import PartitionSpec as P

NPHI = 20480
ROWS = 144
LANES = 256
BLOCK = 256
VMEM_LIMIT = 16 * 1024 * 1024
POINTS_LIMIT = 46 * 1024 * 1024
AHEAD = 4
PARTS = 2
STREAM_LIMIT = 60 * 1024 * 1024
F32 = jnp.float32
BF16 = jnp.bfloat16


def split3(value):
    first = value.astype(BF16).astype(F32)
    rest = value - first
    second = rest.astype(BF16).astype(F32)
    third = (rest - second).astype(BF16).astype(F32)
    return first, second, third


def trig_tables(modes):
    lane = lax.broadcasted_iota(jnp.int32, (64, 128), 1)
    digit = lane & 31
    steps = jnp.where(
        lane < 32, digit * 1024, jnp.where(lane < 64, digit * 32, jnp.where(lane < 96, digit, lane & 3))
    )
    product = modes * steps
    high = product >> 12
    turn = (high - 5 * ((high * 52429) >> 18)) * 4096 + (product & 4095)
    quarter = jnp.zeros_like(turn)
    for edge in (2560, 7680, 12800, 17920):
        quarter = quarter + (turn >= edge).astype(jnp.int32)
    angle = (turn - 5120 * quarter).astype(F32) * (2.0 * math.pi / NPHI)
    quarter = quarter & 3
    sq = angle * angle
    sine = angle * (1.0 + sq * (-1.0 / 6 + sq * (1.0 / 120 + sq * (-1.0 / 5040 + sq * (1.0 / 362880)))))
    cosine = 1.0 + sq * (
        -0.5 + sq * (1.0 / 24 + sq * (-1.0 / 720 + sq * (1.0 / 40320 - sq * (1.0 / 3628800))))
    )
    cos_out = jnp.where(
        quarter == 0, cosine, jnp.where(quarter == 1, -sine, jnp.where(quarter == 2, -cosine, sine))
    )
    sin_out = jnp.where(
        quarter == 0, sine, jnp.where(quarter == 1, cosine, jnp.where(quarter == 2, -sine, -cosine))
    )
    return cos_out, sin_out


def pack_kernel(counts_ref, weights_ref, base_ref, noise_ref, data_ref, blocks_ref):
    data_ref[...] = jnp.zeros_like(data_ref)
    lane = lax.broadcasted_iota(jnp.int32, (24, 128), 1)
    used = jnp.int32(0)
    for owner in range(32):
        count = counts_ref[0, 0, owner]
        pixel = base_ref[1, owner : owner + 1, :] + (owner * 640 - 2)
        if owner == 0:
            pixel = jnp.where(pixel < 0, pixel + NPHI, pixel)
        if owner == 31:
            pixel = jnp.where(pixel >= NPHI, pixel - NPHI, pixel)
        live = jnp.concatenate(
            [
                weights_ref[:, owner, :],
                base_ref[0, owner : owner + 1, :].astype(F32),
                pixel.astype(F32),
                noise_ref[:, owner, :],
                jnp.zeros((4, 128), F32),
            ],
            axis=0,
        )
        live = jnp.where(lane < count, live, 0.0)
        shift = used & 127
        live = pltpu.roll(live, shift, 1)
        start = pl.multiple_of((used >> 7) * 128, 128)
        here = data_ref[:, pl.ds(start, 128)]
        data_ref[:, pl.ds(start, 128)] = jnp.where(lane >= shift, live, here)
        after = pl.multiple_of(start + 128, 128)
        data_ref[:, pl.ds(after, 128)] = jnp.where(lane < shift, live, 0.0)
        used = used + count
    blocks_ref[0] = (used + (BLOCK - 1)) // BLOCK


def points_kernel(
    blocks_ref, sums_ref, x_ref, data_ref, source_ref, out_ref, legendre_ref, table_ref, field_ref, acc_ref, curv_ref, grid_ref, wave_ref, term_ref, hit_ref, sem
):
    move = pltpu.make_async_copy(source_ref, legendre_ref, sem)
    move.start()
    row_id = lax.broadcasted_iota(jnp.int32, (256, 256), 0)
    col_id = lax.broadcasted_iota(jnp.int32, (256, 256), 1)
    to_mode_last = (col_id == 4 * (row_id & 63) + (row_id >> 6)).astype(F32).astype(BF16)
    to_mode_first = (row_id == 4 * (col_id & 63) + (col_id >> 6)).astype(F32).astype(BF16)
    fields = jnp.dot(to_mode_last, x_ref[...], preferred_element_type=F32)
    field_ref[...] = fields.astype(BF16)
    grid_ref[...] = lax.broadcasted_iota(jnp.int32, (ROWS, BLOCK), 0).astype(F32).astype(BF16)
    head = fields[:64, 128:256]
    head_lane = lax.broadcasted_iota(jnp.int32, (64, 128), 1)
    mode_value = jnp.sum(
        jnp.where(head_lane == 4, head * 64.0, jnp.where(head_lane == 5, head, 0.0)),
        axis=1,
        keepdims=True,
    )
    modes = jnp.broadcast_to(mode_value, (64, 128)).astype(jnp.int32)
    cos_tab, sin_tab = trig_tables(modes)
    weight = jnp.where(modes == 0, 1.0, 2.0).astype(F32) * 128.0**-0.5
    lane = lax.broadcasted_iota(jnp.int32, (64, 128), 1)
    groups = [
        (lane < 32, weight),
        ((lane >= 32) & (lane < 64), None),
        ((lane >= 64) & (lane < 96), None),
    ]
    for a in range(4):
        groups.append(((lane >= 96) & (((lane - 96) & 15) >> 2 == a), None))
    for index, (mask, gain) in enumerate(groups):
        for part, table in enumerate((cos_tab, -sin_tab)):
            value = table if gain is None else table * gain
            value = jnp.where(mask, value, 0.0)
            rounded = value.astype(BF16)
            start = (2 * index + part) * 64
            table_ref[pl.ds(start, 64), 0:128] = rounded
            table_ref[pl.ds(start, 64), 128:256] = (value - rounded.astype(F32)).astype(BF16)
    acc_ref[...] = jnp.zeros_like(acc_ref)
    curv_ref[...] = jnp.zeros_like(curv_ref)
    one = jnp.ones((), BF16)
    zero = jnp.zeros((), BF16)

    wave_ref[...] = jnp.zeros_like(wave_ref)
    term_ref[...] = jnp.zeros_like(term_ref)
    hit_ref[...] = jnp.zeros_like(hit_ref)

    def spread():
        acc_ref[:, 0:ROWS] += lax.dot_general(
            term_ref[...], hit_ref[...], (((1,), (1,)), ((), ())), preferred_element_type=F32
        )

    def sample(index):
        start = pl.multiple_of(jnp.maximum(index, 0) * BLOCK, BLOCK)
        info = data_ref[16:24, pl.ds(start, BLOCK)]
        first_row = info[0:1]
        grid_row = grid_ref[...]
        total = [None, None]
        for a in range(4):
            row_hit = jnp.where(grid_row == (first_row + float(a)).astype(BF16), one, zero)
            hit_ref[:, a * BLOCK : (a + 1) * BLOCK] = row_hit
            picked = jnp.dot(field_ref[:, 0:ROWS], row_hit, preferred_element_type=F32)
            wave_re = wave_ref[2 * a]
            wave_im = wave_ref[2 * a + 1]
            for f in range(2):
                term = (
                    picked[128 * f : 128 * f + 64] * wave_re
                    + picked[128 * f + 64 : 128 * f + 128] * wave_im
                )
                total[f] = term if a == 0 else total[f] + term
        weighted = []
        for f in range(2):
            sampled = jnp.sum(total[f], axis=0, keepdims=True)
            value = info[2 + f : 3 + f] * sampled
            curv_ref[f : f + 1, :] += value * sampled
            weighted.append(value)
        for a in range(4):
            for f in range(2):
                for part in range(2):
                    row = 128 * f + 64 * part
                    term_ref[row : row + 64, a * BLOCK : (a + 1) * BLOCK] = (
                        weighted[f] * wave_ref[2 * a + part]
                    ).astype(BF16)

    def turn(index):
        data = data_ref[:, pl.ds(pl.multiple_of(index * BLOCK, BLOCK), BLOCK)]
        pixel = data[17:18].astype(jnp.int32)
        digit_id = grid_ref[0:32, :]
        hit = [
            jnp.where(digit_id == digit.astype(F32).astype(BF16), one, zero)
            for digit in (pixel >> 10, (pixel >> 5) & 31, pixel & 31)
        ]
        weights = data[0:16]
        weights_high = weights.astype(BF16)
        weights_low = (weights - weights_high.astype(F32)).astype(BF16)
        chosen = jnp.concatenate(hit + [weights_high, weights_low], axis=0)
        phases = jnp.dot(
            table_ref[...], jnp.concatenate([chosen, chosen], axis=0), preferred_element_type=F32
        )
        part = [phases[64 * i : 64 * (i + 1)] for i in range(14)]
        mid_re = part[0] * part[2] - part[1] * part[3]
        mid_im = part[0] * part[3] + part[1] * part[2]
        turn_re = mid_re * part[4] - mid_im * part[5]
        turn_im = mid_re * part[5] + mid_im * part[4]
        for a in range(4):
            wave_ref[2 * a] = turn_re * part[6 + 2 * a] - turn_im * part[7 + 2 * a]
            wave_ref[2 * a + 1] = turn_re * part[7 + 2 * a] + turn_im * part[6 + 2 * a]

    def block_step(index, carry):
        spread()
        sample(index - 1)
        turn(index)
        return carry

    lax.fori_loop(0, blocks_ref[0] + 2, block_step, 0)
    back = jnp.dot(to_mode_first, acc_ref[...].astype(BF16), preferred_element_type=F32)
    curvature = jnp.sum(curv_ref[...], axis=(0, 1), keepdims=True) + jnp.sum(
        sums_ref[8:16], axis=(0, 1), keepdims=True
    )
    norm = jnp.sum(sums_ref[0:8], axis=(0, 1), keepdims=True)
    for offset, piece in enumerate(split3(curvature) + split3(norm)):
        back = jnp.where(col_id == 132 + offset, piece, back)
    out_ref[...] = back.astype(BF16)
    move.wait()


def swap_rows(value):
    return jnp.concatenate(
        [
            value[3:4],
            -value[2:3],
            -value[1:2],
            value[0:1],
            value[7:8],
            -value[6:7],
            -value[5:6],
            value[4:5],
        ],
        axis=0,
    )


def scaled_rows(side_ref, beam_ref):
    rows = jnp.concatenate([side_ref[0], side_ref[1]], axis=0)
    return rows, (rows * beam_ref[...]).astype(BF16)


def fetch(source_ref, target_ref, sems, part, m, t):
    chunk = source_ref.shape[2] // sems.shape[0]
    place = pl.ds(part * chunk, chunk)
    return pltpu.make_async_copy(
        source_ref.at[m, t, place], target_ref.at[m, t, place], sems.at[part, m, t]
    )


def start_fetch(source_ref, target_ref, sems, part):
    if part < sems.shape[0]:
        for m in range(2):
            for t in range(2):
                fetch(source_ref, target_ref, sems, part, m, t).start()


def next_part(source_ref, target_ref, sems, part):
    for m in range(2):
        for t in range(2):
            fetch(source_ref, target_ref, sems, part, m, t).wait()
    start_fetch(source_ref, target_ref, sems, part + AHEAD)


def edge_kernel(source_ref, low_ref, high_ref, legendre_ref, sems):
    parts = sems.shape[0]
    chunk = source_ref.shape[2] // parts
    for part in range(AHEAD):
        start_fetch(source_ref, legendre_ref, sems, part)
    row = lax.broadcasted_iota(jnp.int32, (16, 256), 0)
    lane = lax.broadcasted_iota(jnp.int32, (16, 256), 1)
    cycle = (row & 1) + jnp.where(row >= 8, 126, 0)
    picks = []
    for m in range(2):
        pick = (((row >> 1) & 3) == 2 * m + (lane >> 7)) & ((lane & 127) == cycle)
        picks.append(pick.astype(F32).astype(BF16))
    for part in range(parts):
        place = slice(part * chunk, (part + 1) * chunk)
        edges = jnp.zeros((16, chunk), F32)
        next_part(source_ref, legendre_ref, sems, part)
        for m in range(2):
            table = jnp.concatenate([legendre_ref[m, 0, place], legendre_ref[m, 1, place]], axis=1)
            edges = edges + lax.dot_general(
                picks[m], table, (((1,), (1,)), ((), ())), preferred_element_type=F32
            )
        high_ref[:, place] = edges[0:8].astype(BF16)
        low_ref[:, place] = edges[8:16].astype(BF16)


def synth_kernel(side_ref, beam_ref, spectra_ref, legendre_ref, modes_ref, sums_ref):
    rows, coef = scaled_rows(side_ref, beam_ref)
    square = rows * rows
    spectra = spectra_ref[...]
    pair = jnp.concatenate([spectra[0:1]] * 2 + [spectra[1:2]] * 2, axis=0)
    prior = square * jnp.concatenate([pair, pair], axis=0)
    norm_sum = square[:, 0:128]
    prior_sum = prior[:, 0:128]
    for start in range(128, rows.shape[1], 128):
        norm_sum = norm_sum + square[:, start : start + 128]
        prior_sum = prior_sum + prior[:, start : start + 128]
    sums_ref[...] = jnp.concatenate([norm_sum, prior_sum], axis=0) * 0.125
    own = []
    for m in range(2):
        table = jnp.concatenate([legendre_ref[m, 0], legendre_ref[m, 1]], axis=1)
        own.append(jnp.dot(coef, table, preferred_element_type=F32)[4 * m : 4 * m + 4])
    modes_ref[...] = jnp.concatenate(own, axis=0)


def fields_kernel(m_ref, side_ref, beam_ref, low_ref, high_ref, modes_ref, out_ref):
    _, coef = scaled_rows(side_ref, beam_ref)
    rims = jnp.concatenate([low_ref[...], high_ref[...]], axis=0)
    rim = lax.dot_general(coef, rims, (((1,), (1,)), ((), ())), preferred_element_type=F32)
    rim = jnp.concatenate([rim, jnp.zeros((8, 112), F32)], axis=1)
    row = lax.broadcasted_iota(jnp.int32, (8, 128), 0)
    lane = lax.broadcasted_iota(jnp.int32, (8, 128), 1)
    rim = jnp.where(row < 4, rim, pltpu.roll(rim, 124, 1))
    low, high = [], []
    for t in range(2):
        own = pltpu.roll(modes_ref[:, 128 * t : 128 * t + 128], 2, 1)
        below = pltpu.roll(rim, 126, 1) if t else rim
        above = pltpu.roll(rim, 120 if t else 122, 1)
        low.append(jnp.where(lane < 2, below, own))
        high.append(jnp.where(lane < 2, own, jnp.where(lane < 4, above, 0.0)))
    low = swap_rows(low[1]) - low[0]
    high = swap_rows(high[1]) - high[0]
    mode = jnp.where(row < 4, m_ref[0], m_ref[1])
    high = jnp.where(lane == 4, (mode >> 6).astype(F32), high)
    high = jnp.where(lane == 5, (mode & 63).astype(F32), high)
    sent = jnp.concatenate([low, high], axis=1).astype(BF16)
    for target in range(32):
        out_ref[target] = sent


def analysis_kernel(got_ref, low_ref, high_ref, legendre_ref, out_ref):
    total = got_ref[0].astype(F32)
    for source in range(1, 32):
        total = total + got_ref[source].astype(F32)
    lane = lax.broadcasted_iota(jnp.int32, (8, 128), 1)
    row = lax.broadcasted_iota(jnp.int32, (8, 128), 0)
    low, high = total[:, 0:128], total[:, 128:256]
    curvature = jnp.sum(jnp.where((lane >= 4) & (lane < 7), high, 0.0), axis=1, keepdims=True)
    norm = jnp.sum(jnp.where((lane >= 7) & (lane < 10), high, 0.0), axis=1, keepdims=True)
    sums = jnp.where(lane == 0, curvature, jnp.where(lane == 1, norm, 0.0))
    own = jnp.where(lane < 126, pltpu.roll(low, 126, 1), pltpu.roll(high, 126, 1))
    own_both = jnp.concatenate([-own, swap_rows(own)], axis=1)
    row_both = lax.broadcasted_iota(jnp.int32, (8, 256), 0)
    owns = []
    for m in range(2):
        owns.append(jnp.where((row_both >> 2) == m, own_both, 0.0).astype(BF16))
    low_swap, high_swap = swap_rows(low), swap_rows(high)
    rim = jnp.where(lane < 2, -low, jnp.where(lane < 4, pltpu.roll(low_swap, 2, 1), 0.0))
    rim = jnp.where((lane >= 8) & (lane < 10), pltpu.roll(-high, 6, 1), rim)
    rim = jnp.where((lane >= 10) & (lane < 12), pltpu.roll(high_swap, 8, 1), rim)
    rim = jnp.where(row < 4, rim, pltpu.roll(rim, 4, 1)).astype(BF16)


    bands = out_ref.shape[0]
    chunk = legendre_ref.shape[2] // bands
    for band in range(bands):
        place = slice(band * chunk, (band + 1) * chunk)
        rims = jnp.concatenate([low_ref[:, place], high_ref[:, place]], axis=0)
        result = jnp.dot(rim[:, 0:16], rims, preferred_element_type=F32)
        for m in range(2):
            table = jnp.concatenate([legendre_ref[m, 0, place], legendre_ref[m, 1, place]], axis=1)
            result = result + lax.dot_general(
                owns[m], table, (((1,), (1,)), ((), ())), preferred_element_type=F32
            )
        out_ref[band, :, 0:chunk] = result
        out_ref[band, :, chunk : chunk + 128] = sums


def update_kernel(band_ref, parts_ref, side_ref, beam_ref, spectra_ref, solution_ref, residual_ref):
    del band_ref
    total = parts_ref[0]
    for source in range(1, parts_ref.shape[0]):
        total = total + parts_ref[source]
    share = side_ref.shape[2]
    step = total[0:1, share + 1 : share + 2] / total[0:1, share : share + 1]
    spectra = spectra_ref[...]
    pair = jnp.concatenate([spectra[0:1]] * 2 + [spectra[1:2]] * 2, axis=0)
    beam = beam_ref[...]
    for m in range(2):
        side = side_ref[m]
        image = pair * side + beam * total[4 * m : 4 * m + 4, 0:share]
        solution_ref[m] = step * side
        residual_ref[m] = side - step * image


def local(
    right_side,
    inv_spectra,
    beam,
    m_values,
    legendre,
    stencil_weights,
    stencil_base,
    inv_noise,
    slot_counts,
):
    band_count = lax.axis_size("band")
    lmax_len = right_side.shape[2]
    share_len = lmax_len // band_count
    smem = pl.BlockSpec(memory_space=pltpu.SMEM)
    vmem = pl.BlockSpec(memory_space=pltpu.VMEM)
    params = pltpu.CompilerParams(vmem_limit_bytes=VMEM_LIMIT)
    stream_params = pltpu.CompilerParams(vmem_limit_bytes=STREAM_LIMIT)
    hbm = pl.BlockSpec(memory_space=pl.ANY)
    beam_row = beam.reshape(1, lmax_len)

    low_edge, high_edge = pl.pallas_call(
        edge_kernel,
        out_shape=(
            jax.ShapeDtypeStruct((8, lmax_len), BF16),
            jax.ShapeDtypeStruct((8, lmax_len), BF16),
        ),
        in_specs=[hbm],
        out_specs=(vmem, vmem),
        scratch_shapes=[pltpu.VMEM(legendre.shape, BF16), pltpu.SemaphoreType.DMA((PARTS, 2, 2))],
        compiler_params=stream_params,
        name="edges",
    )(legendre)
    own_modes, sums = pl.pallas_call(
        synth_kernel,
        out_shape=(
            jax.ShapeDtypeStruct((8, 256), F32),
            jax.ShapeDtypeStruct((16, 128), F32),
        ),
        in_specs=[vmem, vmem, vmem, vmem],
        out_specs=(vmem, vmem),
        compiler_params=params,
        cost_estimate=pl.CostEstimate(flops=10**7, bytes_accessed=6 * 10**6, transcendentals=0),
        name="synth",
    )(right_side, beam_row, inv_spectra, legendre)
    up = [(i, i + 1) for i in range(band_count - 1)]
    down = [(i + 1, i) for i in range(band_count - 1)]
    low_rim = lax.ppermute(low_edge, "band", up)
    high_rim = lax.ppermute(high_edge, "band", down)

    data, blocks = pl.pallas_call(
        pack_kernel,
        out_shape=(
            jax.ShapeDtypeStruct((24, 4096 + 128 + 3 * BLOCK), F32),
            jax.ShapeDtypeStruct((1,), jnp.int32),
        ),
        in_specs=[smem, vmem, vmem, vmem],
        out_specs=(vmem, smem),
        compiler_params=params,
        cost_estimate=pl.CostEstimate(flops=10**6, bytes_accessed=3 * 10**6, transcendentals=0),
        name="pack",
    )(
        slot_counts,
        stencil_weights.reshape(16, 32, 128),
        stencil_base.reshape(2, 32, 128),
        inv_noise.reshape(2, 32, 128),
    )

    sent = pl.pallas_call(
        fields_kernel,
        out_shape=jax.ShapeDtypeStruct((32, 8, LANES), BF16),
        in_specs=[smem, vmem, vmem, vmem, vmem, vmem],
        out_specs=vmem,
        compiler_params=params,
        name="fields",
    )(m_values, right_side, beam_row, low_rim, high_rim, own_modes)
    got = lax.all_to_all(sent, "harm", split_axis=0, concat_axis=0, tiled=True)

    back, table = pl.pallas_call(
        points_kernel,
        out_shape=(
            jax.ShapeDtypeStruct((256, LANES), BF16),
            jax.ShapeDtypeStruct(legendre.shape, BF16),
        ),
        in_specs=[smem, vmem, vmem, vmem, hbm],
        out_specs=(vmem, vmem),
        scratch_shapes=[
            pltpu.VMEM((896, 256), BF16),
            pltpu.VMEM((256, LANES), BF16),
            pltpu.VMEM((256, LANES), F32),
            pltpu.VMEM((2, BLOCK), F32),
            pltpu.VMEM((ROWS, BLOCK), BF16),
            pltpu.VMEM((8, 64, BLOCK), F32),
            pltpu.VMEM((256, 4 * BLOCK), BF16),
            pltpu.VMEM((ROWS, 4 * BLOCK), BF16),
            pltpu.SemaphoreType.DMA(()),
        ],
        compiler_params=pltpu.CompilerParams(vmem_limit_bytes=POINTS_LIMIT),
        name="points",
    )(blocks, sums, got.reshape(256, LANES), data, legendre)
    back_got = lax.all_to_all(
        back.reshape(32, 8, LANES), "harm", split_axis=0, concat_axis=0, tiled=True
    )

    harmonic = pl.pallas_call(
        analysis_kernel,
        out_shape=jax.ShapeDtypeStruct((band_count, 8, share_len + 128), F32),
        in_specs=[vmem, vmem, vmem, vmem],
        out_specs=vmem,
        compiler_params=params,
        name="analysis",
    )(back_got, low_rim, high_rim, table)
    parts = lax.all_to_all(harmonic, "band", split_axis=0, concat_axis=0, tiled=True)

    band = lax.axis_index("band").astype(jnp.int32).reshape(1)
    return pl.pallas_call(
        update_kernel,
        grid_spec=pltpu.PrefetchScalarGridSpec(
            num_scalar_prefetch=1,
            grid=(1,),
            in_specs=[
                pl.BlockSpec((band_count, 8, share_len + 128), lambda i, b: (0, 0, 0)),
                pl.BlockSpec((2, 4, share_len), lambda i, b: (0, 0, b[0])),
                pl.BlockSpec((1, share_len), lambda i, b: (0, b[0])),
                pl.BlockSpec((2, share_len), lambda i, b: (0, b[0])),
            ],
            out_specs=(
                pl.BlockSpec((2, 4, share_len), lambda i, b: (0, 0, 0)),
                pl.BlockSpec((2, 4, share_len), lambda i, b: (0, 0, 0)),
            ),
        ),
        out_shape=(
            jax.ShapeDtypeStruct((2, 4, share_len), F32),
            jax.ShapeDtypeStruct((2, 4, share_len), F32),
        ),
        compiler_params=params,
        name="update",
    )(band, parts, right_side, beam_row, inv_spectra)


def solution(mesh):
    placed = (
        P("harm", None, None),
        P(),
        P(),
        P("harm"),
        P("harm", None, None, "band"),
        P(None, "harm", "band", None, None),
        P(None, "harm", "band", None, None),
        P(None, "harm", "band", None, None),
        P("harm", "band", None),
    )
    return jax.shard_map(
        local,
        mesh=mesh,
        in_specs=placed,
        out_specs=(P("harm", None, "band"), P("harm", None, "band")),
        check_vma=False,
    )
```

```python
import functools
import math

import jax
import jax.numpy as jnp
from jax import lax
from jax.experimental import pallas as pl
from jax.experimental.pallas import tpu as pltpu
from jax.sharding import PartitionSpec as P

NPHI = 20480
ROWS = 144
LANES = 256
PIECE = 640
BLOCK = 256
VMEM_LIMIT = 16 * 1024 * 1024
AHEAD = 4
PARTS = 2
STREAM_LIMIT = 46 * 1024 * 1024
F32 = jnp.float32
BF16 = jnp.bfloat16


def split3(value):
    first = value.astype(BF16).astype(F32)
    rest = value - first
    second = rest.astype(BF16).astype(F32)
    third = (rest - second).astype(BF16).astype(F32)
    return first, second, third


def trig_tables(modes):
    lane = lax.broadcasted_iota(jnp.int32, (64, 128), 1)
    digit = lane & 31
    steps = jnp.where(
        lane < 32, digit * 1024, jnp.where(lane < 64, digit * 32, jnp.where(lane < 96, digit, lane & 3))
    )
    product = modes * steps
    high = product >> 12
    turn = (high - 5 * ((high * 52429) >> 18)) * 4096 + (product & 4095)
    quarter = jnp.zeros_like(turn)
    for edge in (2560, 7680, 12800, 17920):
        quarter = quarter + (turn >= edge).astype(jnp.int32)
    angle = (turn - 5120 * quarter).astype(F32) * (2.0 * math.pi / NPHI)
    quarter = quarter & 3
    sq = angle * angle
    sine = angle * (1.0 + sq * (-1.0 / 6 + sq * (1.0 / 120 + sq * (-1.0 / 5040 + sq * (1.0 / 362880)))))
    cosine = 1.0 + sq * (
        -0.5 + sq * (1.0 / 24 + sq * (-1.0 / 720 + sq * (1.0 / 40320 - sq * (1.0 / 3628800))))
    )
    cos_out = jnp.where(
        quarter == 0, cosine, jnp.where(quarter == 1, -sine, jnp.where(quarter == 2, -cosine, sine))
    )
    sin_out = jnp.where(
        quarter == 0, sine, jnp.where(quarter == 1, cosine, jnp.where(quarter == 2, -sine, -cosine))
    )
    return cos_out, sin_out


def pack_kernel(counts_ref, weights_ref, base_ref, noise_ref, data_ref, blocks_ref):
    data_ref[...] = jnp.zeros_like(data_ref)
    lane = lax.broadcasted_iota(jnp.int32, (24, 128), 1)
    used = jnp.int32(0)
    for owner in range(32):
        count = counts_ref[0, 0, owner]
        pixel = base_ref[1, owner : owner + 1, :] + (owner * 640 - 2)
        if owner == 0:
            pixel = jnp.where(pixel < 0, pixel + NPHI, pixel)
        if owner == 31:
            pixel = jnp.where(pixel >= NPHI, pixel - NPHI, pixel)
        live = jnp.concatenate(
            [
                weights_ref[:, owner, :],
                base_ref[0, owner : owner + 1, :].astype(F32),
                pixel.astype(F32),
                noise_ref[:, owner, :],
                jnp.zeros((4, 128), F32),
            ],
            axis=0,
        )
        live = jnp.where(lane < count, live, 0.0)
        shift = used & 127
        live = pltpu.roll(live, shift, 1)
        start = pl.multiple_of((used >> 7) * 128, 128)
        here = data_ref[:, pl.ds(start, 128)]
        data_ref[:, pl.ds(start, 128)] = jnp.where(lane >= shift, live, here)
        after = pl.multiple_of(start + 128, 128)
        data_ref[:, pl.ds(after, 128)] = jnp.where(lane < shift, live, 0.0)
        used = used + count
    blocks_ref[0] = (used + (BLOCK - 1)) // BLOCK


def to_pieces(low, high, extra, first, count):
    lane = lax.broadcasted_iota(jnp.int32, low[0].shape, 1)
    rest = jnp.where((lane >= 16) & (lane < 16 + count), pltpu.roll(extra, 16 - first, 1), 0.0)
    for q in range(4):
        moved = pltpu.roll(high[q], 4 * q, 1) if q else high[q]
        rest = jnp.where((lane >= 4 * q) & (lane < 4 * q + 4), moved, rest)
    return jnp.concatenate(low + [rest], axis=1)


def points_kernel(
    blocks_ref, sums_ref, x_ref, data_ref, source_ref, out_ref, legendre_ref, table_ref, field_ref, acc_ref, curv_ref, grid_ref, wave_ref, term_ref, hit_ref, sem
):
    move = pltpu.make_async_copy(source_ref, legendre_ref, sem)
    move.start()
    got = jnp.concatenate([x_ref[source].astype(F32) for source in range(32)], axis=0)
    rest = got[:, 512:640]
    lane = lax.broadcasted_iota(jnp.int32, (64, 128), 1)
    for q in range(4):
        rows = slice(64 * q, 64 * q + 64)
        field_ref[rows, 0:128] = got[:, 128 * q : 128 * q + 128].astype(BF16)
        moved = pltpu.roll(rest, 128 - 4 * q, 1) if q else rest
        field_ref[rows, 128:256] = jnp.where(lane < 4, moved, 0.0).astype(BF16)
    grid_ref[...] = lax.broadcasted_iota(jnp.int32, (ROWS, BLOCK), 0).astype(F32).astype(BF16)
    mode_value = jnp.sum(
        jnp.where(lane == 16, rest * 64.0, jnp.where(lane == 17, rest, 0.0)), axis=1, keepdims=True
    )
    modes = jnp.broadcast_to(mode_value, (64, 128)).astype(jnp.int32)
    cos_tab, sin_tab = trig_tables(modes)
    weight = jnp.where(modes == 0, 1.0, 2.0).astype(F32) * 128.0**-0.5
    groups = [
        (lane < 32, weight),
        ((lane >= 32) & (lane < 64), None),
        ((lane >= 64) & (lane < 96), None),
    ]
    for a in range(4):
        groups.append(((lane >= 96) & (((lane - 96) & 15) >> 2 == a), None))
    for index, (mask, gain) in enumerate(groups):
        for part, table in enumerate((cos_tab, -sin_tab)):
            value = table if gain is None else table * gain
            value = jnp.where(mask, value, 0.0)
            rounded = value.astype(BF16)
            start = (2 * index + part) * 64
            table_ref[pl.ds(start, 64), 0:128] = rounded
            table_ref[pl.ds(start, 64), 128:256] = (value - rounded.astype(F32)).astype(BF16)
    acc_ref[...] = jnp.zeros_like(acc_ref)
    curv_ref[...] = jnp.zeros_like(curv_ref)
    one = jnp.ones((), BF16)
    zero = jnp.zeros((), BF16)

    term_ref[...] = jnp.zeros_like(term_ref)
    hit_ref[...] = jnp.zeros_like(hit_ref)

    def spread():
        acc_ref[:, 0:ROWS] += lax.dot_general(
            term_ref[...], hit_ref[...], (((1,), (1,)), ((), ())), preferred_element_type=F32
        )

    def sample(index):
        start = pl.multiple_of(index * BLOCK, BLOCK)
        info = data_ref[16:24, pl.ds(start, BLOCK)]
        first_row = info[0:1]
        grid_row = grid_ref[...]
        total = [None, None]
        for a in range(4):
            row_hit = jnp.where(grid_row == (first_row + float(a)).astype(BF16), one, zero)
            hit_ref[:, a * BLOCK : (a + 1) * BLOCK] = row_hit
            picked = jnp.dot(field_ref[:, 0:ROWS], row_hit, preferred_element_type=F32)
            wave_re = wave_ref[2 * a]
            wave_im = wave_ref[2 * a + 1]
            for f in range(2):
                term = (
                    picked[128 * f : 128 * f + 64] * wave_re
                    + picked[128 * f + 64 : 128 * f + 128] * wave_im
                )
                total[f] = term if a == 0 else total[f] + term
        weighted = []
        for f in range(2):
            sampled = jnp.sum(total[f], axis=0, keepdims=True)
            value = info[2 + f : 3 + f] * sampled
            curv_ref[f : f + 1, :] += value * sampled
            weighted.append(value)
        for a in range(4):
            for f in range(2):
                for part in range(2):
                    row = 128 * f + 64 * part
                    term_ref[row : row + 64, a * BLOCK : (a + 1) * BLOCK] = (
                        weighted[f] * wave_ref[2 * a + part]
                    ).astype(BF16)

    def turn(index):
        data = data_ref[:, pl.ds(pl.multiple_of(index * BLOCK, BLOCK), BLOCK)]
        pixel = data[17:18].astype(jnp.int32)
        digit_id = grid_ref[0:32, :]
        hit = [
            jnp.where(digit_id == digit.astype(F32).astype(BF16), one, zero)
            for digit in (pixel >> 10, (pixel >> 5) & 31, pixel & 31)
        ]
        weights = data[0:16]
        weights_high = weights.astype(BF16)
        weights_low = (weights - weights_high.astype(F32)).astype(BF16)
        chosen = jnp.concatenate(hit + [weights_high, weights_low], axis=0)
        phases = jnp.dot(
            table_ref[...], jnp.concatenate([chosen, chosen], axis=0), preferred_element_type=F32
        )
        part = [phases[64 * i : 64 * (i + 1)] for i in range(14)]
        mid_re = part[0] * part[2] - part[1] * part[3]
        mid_im = part[0] * part[3] + part[1] * part[2]
        turn_re = mid_re * part[4] - mid_im * part[5]
        turn_im = mid_re * part[5] + mid_im * part[4]
        for a in range(4):
            wave_ref[2 * a] = turn_re * part[6 + 2 * a] - turn_im * part[7 + 2 * a]
            wave_ref[2 * a + 1] = turn_re * part[7 + 2 * a] + turn_im * part[6 + 2 * a]

    def block_step(index, carry):
        spread()
        sample(index)
        turn(index + 1)
        return carry

    turn(0)
    lax.fori_loop(0, blocks_ref[0], block_step, 0)
    spread()
    curvature = jnp.sum(curv_ref[...], axis=(0, 1), keepdims=True) + jnp.sum(
        sums_ref[8:16], axis=(0, 1), keepdims=True
    )
    norm = jnp.sum(sums_ref[0:8], axis=(0, 1), keepdims=True)
    extra = jnp.zeros((64, 128), F32)
    for offset, piece in enumerate(split3(curvature) + split3(norm)):
        extra = jnp.where(lane == offset, piece, extra)
    back = [acc_ref[64 * q : 64 * q + 64] for q in range(4)]
    sent = to_pieces([b[:, 0:128] for b in back], [b[:, 128:256] for b in back], extra, 0, 6)
    for target in range(32):
        out_ref[target] = sent[2 * target : 2 * target + 2].astype(BF16)
    move.wait()


def swap_rows(value):
    return jnp.concatenate(
        [
            value[3:4],
            -value[2:3],
            -value[1:2],
            value[0:1],
            value[7:8],
            -value[6:7],
            -value[5:6],
            value[4:5],
        ],
        axis=0,
    )


def scaled_rows(side_ref, beam_ref):
    rows = jnp.concatenate([side_ref[0], side_ref[1]], axis=0)
    return rows, (rows * beam_ref[...]).astype(BF16)


def fetch(source_ref, target_ref, sems, part, m, t):
    chunk = source_ref.shape[2] // sems.shape[0]
    place = pl.ds(part * chunk, chunk)
    return pltpu.make_async_copy(
        source_ref.at[m, t, place], target_ref.at[m, t, place], sems.at[part, m, t]
    )


def start_fetch(source_ref, target_ref, sems, part):
    if part < sems.shape[0]:
        for m in range(2):
            for t in range(2):
                fetch(source_ref, target_ref, sems, part, m, t).start()


def next_part(source_ref, target_ref, sems, part):
    for m in range(2):
        for t in range(2):
            fetch(source_ref, target_ref, sems, part, m, t).wait()
    start_fetch(source_ref, target_ref, sems, part + AHEAD)


def edge_kernel(source_ref, low_ref, high_ref, legendre_ref, sems):
    parts = sems.shape[0]
    chunk = source_ref.shape[2] // parts
    for part in range(AHEAD):
        start_fetch(source_ref, legendre_ref, sems, part)
    row = lax.broadcasted_iota(jnp.int32, (16, 256), 0)
    lane = lax.broadcasted_iota(jnp.int32, (16, 256), 1)
    cycle = (row & 1) + jnp.where(row >= 8, 126, 0)
    picks = []
    for m in range(2):
        pick = (((row >> 1) & 3) == 2 * m + (lane >> 7)) & ((lane & 127) == cycle)
        picks.append(pick.astype(F32).astype(BF16))
    for part in range(parts):
        place = slice(part * chunk, (part + 1) * chunk)
        edges = jnp.zeros((16, chunk), F32)
        next_part(source_ref, legendre_ref, sems, part)
        for m in range(2):
            table = jnp.concatenate([legendre_ref[m, 0, place], legendre_ref[m, 1, place]], axis=1)
            edges = edges + lax.dot_general(
                picks[m], table, (((1,), (1,)), ((), ())), preferred_element_type=F32
            )
        high_ref[:, place] = edges[0:8].astype(BF16)
        low_ref[:, place] = edges[8:16].astype(BF16)


def synth_kernel(
    m_ref, side_ref, beam_ref, spectra_ref, legendre_ref, own_ref, coef_ref, sums_ref
):
    rows, coef = scaled_rows(side_ref, beam_ref)
    square = rows * rows
    spectra = spectra_ref[...]
    pair = jnp.concatenate([spectra[0:1]] * 2 + [spectra[1:2]] * 2, axis=0)
    prior = square * jnp.concatenate([pair, pair], axis=0)
    norm_sum = square[:, 0:128]
    prior_sum = prior[:, 0:128]
    for start in range(128, rows.shape[1], 128):
        norm_sum = norm_sum + square[:, start : start + 128]
        prior_sum = prior_sum + prior[:, start : start + 128]
    sums_ref[...] = jnp.concatenate([norm_sum, prior_sum], axis=0) * 0.125
    own = []
    for m in range(2):
        table = jnp.concatenate([legendre_ref[m, 0], legendre_ref[m, 1]], axis=1)
        own.append(jnp.dot(coef, table, preferred_element_type=F32)[4 * m : 4 * m + 4])
    modes = jnp.concatenate(own, axis=0)
    fields = pltpu.roll(swap_rows(modes[:, 128:256]) - modes[:, 0:128], 2, 1)
    row = lax.broadcasted_iota(jnp.int32, (8, 128), 0)
    lane = lax.broadcasted_iota(jnp.int32, (8, 128), 1)
    own_ref[0:8] = jnp.where(lane < 2, 0.0, fields)
    mode = jnp.where(row < 4, m_ref[0], m_ref[1])
    high = jnp.where(lane < 2, fields, 0.0)
    high = jnp.where(lane == 4, (mode >> 6).astype(F32), high)
    own_ref[8:16] = jnp.where(lane == 5, (mode & 63).astype(F32), high)
    coef_ref[...] = coef


def both_modes(value, q):
    return jnp.concatenate([value[q : q + 1], value[q + 4 : q + 5]], axis=0)


def fields_kernel(coef_ref, low_ref, high_ref, own_ref, out_ref):
    rims = jnp.concatenate([low_ref[...], high_ref[...]], axis=0)
    rim = lax.dot_general(
        coef_ref[...], rims, (((1,), (1,)), ((), ())), preferred_element_type=F32
    )
    rim = jnp.concatenate([rim, jnp.zeros((8, 112), F32)], axis=1)
    row = lax.broadcasted_iota(jnp.int32, (8, 128), 0)
    lane = lax.broadcasted_iota(jnp.int32, (8, 128), 1)
    rim = jnp.where(row < 4, rim, pltpu.roll(rim, 124, 1))
    rim = swap_rows(pltpu.roll(rim, 126, 1)) - rim
    low = jnp.where(lane < 2, rim, own_ref[0:8])
    high = jnp.where((lane == 2) | (lane == 3), pltpu.roll(rim, 122, 1), own_ref[8:16])
    sent = to_pieces([both_modes(low, q) for q in range(4)], [both_modes(high, q) for q in range(4)], both_modes(high, 0), 4, 2)
    sent = sent.astype(BF16)
    for target in range(32):
        out_ref[target] = sent


def analysis_kernel(got_ref, low_ref, high_ref, legendre_ref, out_ref):
    total = got_ref[0].astype(F32)
    for source in range(1, 32):
        total = total + got_ref[source].astype(F32)
    lane = lax.broadcasted_iota(jnp.int32, (8, 128), 1)
    row = lax.broadcasted_iota(jnp.int32, (8, 128), 0)
    rest = total[:, 512:640]
    low = jnp.concatenate(
        [total[m : m + 1, 128 * q : 128 * q + 128] for m in range(2) for q in range(4)], axis=0
    )
    moved = [pltpu.roll(rest, 128 - 4 * q, 1) if q else rest for q in range(4)]
    high = jnp.concatenate([moved[q][m : m + 1] for m in range(2) for q in range(4)], axis=0)
    extra = jnp.broadcast_to(rest[0:1], (8, 128))
    curvature = jnp.sum(
        jnp.where((lane >= 16) & (lane < 19), extra, 0.0), axis=1, keepdims=True
    )
    norm = jnp.sum(jnp.where((lane >= 19) & (lane < 22), extra, 0.0), axis=1, keepdims=True)
    sums = jnp.where(lane == 0, curvature, jnp.where(lane == 1, norm, 0.0))
    own = jnp.where(lane < 126, pltpu.roll(low, 126, 1), pltpu.roll(high, 126, 1))
    own_both = jnp.concatenate([-own, swap_rows(own)], axis=1)
    row_both = lax.broadcasted_iota(jnp.int32, (8, 256), 0)
    owns = []
    for m in range(2):
        owns.append(jnp.where((row_both >> 2) == m, own_both, 0.0).astype(BF16))
    low_swap, high_swap = swap_rows(low), swap_rows(high)
    rim = jnp.where(lane < 2, -low, jnp.where(lane < 4, pltpu.roll(low_swap, 2, 1), 0.0))
    rim = jnp.where((lane >= 8) & (lane < 10), pltpu.roll(-high, 6, 1), rim)
    rim = jnp.where((lane >= 10) & (lane < 12), pltpu.roll(high_swap, 8, 1), rim)
    rim = jnp.where(row < 4, rim, pltpu.roll(rim, 4, 1)).astype(BF16)


    bands = out_ref.shape[0]
    chunk = legendre_ref.shape[2] // bands
    for band in range(bands):
        place = slice(band * chunk, (band + 1) * chunk)
        rims = jnp.concatenate([low_ref[:, place], high_ref[:, place]], axis=0)
        result = jnp.dot(rim[:, 0:16], rims, preferred_element_type=F32)
        for m in range(2):
            table = jnp.concatenate([legendre_ref[m, 0, place], legendre_ref[m, 1, place]], axis=1)
            result = result + lax.dot_general(
                owns[m], table, (((1,), (1,)), ((), ())), preferred_element_type=F32
            )
        out_ref[band, :, 0:chunk] = result
        out_ref[band, :, chunk : chunk + 128] = sums


def update_kernel(band_ref, parts_ref, side_ref, beam_ref, spectra_ref, solution_ref, residual_ref):
    del band_ref
    total = parts_ref[0]
    for source in range(1, parts_ref.shape[0]):
        total = total + parts_ref[source]
    share = side_ref.shape[2]
    step = total[0:1, share + 1 : share + 2] / total[0:1, share : share + 1]
    spectra = spectra_ref[...]
    pair = jnp.concatenate([spectra[0:1]] * 2 + [spectra[1:2]] * 2, axis=0)
    beam = beam_ref[...]
    for m in range(2):
        side = side_ref[m]
        image = pair * side + beam * total[4 * m : 4 * m + 4, 0:share]
        solution_ref[m] = step * side
        residual_ref[m] = side - step * image


def local(
    right_side,
    inv_spectra,
    beam,
    m_values,
    legendre,
    stencil_weights,
    stencil_base,
    inv_noise,
    slot_counts,
):
    band_count = lax.axis_size("band")
    lmax_len = right_side.shape[2]
    share_len = lmax_len // band_count
    smem = pl.BlockSpec(memory_space=pltpu.SMEM)
    vmem = pl.BlockSpec(memory_space=pltpu.VMEM)
    params = pltpu.CompilerParams(vmem_limit_bytes=VMEM_LIMIT)
    stream_params = pltpu.CompilerParams(vmem_limit_bytes=STREAM_LIMIT)
    hbm = pl.BlockSpec(memory_space=pl.ANY)
    beam_row = beam.reshape(1, lmax_len)

    low_edge, high_edge, near_table = pl.pallas_call(
        edge_kernel,
        out_shape=(
            jax.ShapeDtypeStruct((8, lmax_len), BF16),
            jax.ShapeDtypeStruct((8, lmax_len), BF16),
            jax.ShapeDtypeStruct(legendre.shape, BF16),
        ),
        in_specs=[hbm],
        out_specs=(vmem, vmem, vmem),
        scratch_shapes=[pltpu.SemaphoreType.DMA((PARTS, 2, 2))],
        compiler_params=stream_params,
        name="edges",
    )(legendre)
    own_fields, coef, sums = pl.pallas_call(
        synth_kernel,
        out_shape=(
            jax.ShapeDtypeStruct((16, 128), F32),
            jax.ShapeDtypeStruct((8, lmax_len), BF16),
            jax.ShapeDtypeStruct((16, 128), F32),
        ),
        in_specs=[smem, vmem, vmem, vmem, vmem],
        out_specs=(vmem, vmem, vmem),
        compiler_params=params,
        cost_estimate=pl.CostEstimate(flops=10**7, bytes_accessed=6 * 10**6, transcendentals=0),
        name="synth",
    )(m_values, right_side, beam_row, inv_spectra, near_table)
    up = [(i, i + 1) for i in range(band_count - 1)]
    down = [(i + 1, i) for i in range(band_count - 1)]
    low_rim = lax.ppermute(low_edge, "band", up)
    high_rim = lax.ppermute(high_edge, "band", down)

    data, blocks = pl.pallas_call(
        pack_kernel,
        out_shape=(
            jax.ShapeDtypeStruct((24, 4096 + 128 + 3 * BLOCK), F32),
            jax.ShapeDtypeStruct((1,), jnp.int32),
        ),
        in_specs=[smem, vmem, vmem, vmem],
        out_specs=(vmem, smem),
        compiler_params=params,
        cost_estimate=pl.CostEstimate(flops=10**6, bytes_accessed=3 * 10**6, transcendentals=0),
        name="pack",
    )(
        slot_counts,
        stencil_weights.reshape(16, 32, 128),
        stencil_base.reshape(2, 32, 128),
        inv_noise.reshape(2, 32, 128),
    )

    sent = pl.pallas_call(
        fields_kernel,
        out_shape=jax.ShapeDtypeStruct((32, 2, PIECE), BF16),
        in_specs=[vmem, vmem, vmem, vmem],
        out_specs=vmem,
        compiler_params=params,
        name="fields",
    )(coef, low_rim, high_rim, own_fields)
    band = lax.axis_index("band").astype(jnp.int32).reshape(1)
    got = lax.all_to_all(sent, "harm", split_axis=0, concat_axis=0, tiled=True)

    back, table = pl.pallas_call(
        points_kernel,
        out_shape=(
            jax.ShapeDtypeStruct((32, 2, PIECE), BF16),
            jax.ShapeDtypeStruct(legendre.shape, BF16),
        ),
        in_specs=[smem, vmem, vmem, vmem, hbm],
        out_specs=(vmem, vmem),
        scratch_shapes=[
            pltpu.VMEM((896, 256), BF16),
            pltpu.VMEM((256, LANES), BF16),
            pltpu.VMEM((256, LANES), F32),
            pltpu.VMEM((2, BLOCK), F32),
            pltpu.VMEM((ROWS, BLOCK), BF16),
            pltpu.VMEM((8, 64, BLOCK), F32),
            pltpu.VMEM((256, 4 * BLOCK), BF16),
            pltpu.VMEM((ROWS, 4 * BLOCK), BF16),
            pltpu.SemaphoreType.DMA(()),
        ],
        compiler_params=stream_params,
        name="points",
    )(blocks, sums, got, data, legendre)
    back, band = lax.optimization_barrier((back, band))
    back_got = lax.all_to_all(back, "harm", split_axis=0, concat_axis=0, tiled=True)

    harmonic = pl.pallas_call(
        analysis_kernel,
        out_shape=jax.ShapeDtypeStruct((band_count, 8, share_len + 128), F32),
        in_specs=[vmem, vmem, vmem, vmem],
        out_specs=vmem,
        compiler_params=params,
        name="analysis",
    )(back_got, low_rim, high_rim, table)
    parts = lax.all_to_all(harmonic, "band", split_axis=0, concat_axis=0, tiled=True)

    return pl.pallas_call(
        update_kernel,
        grid_spec=pltpu.PrefetchScalarGridSpec(
            num_scalar_prefetch=1,
            grid=(1,),
            in_specs=[
                pl.BlockSpec((band_count, 8, share_len + 128), lambda i, b: (0, 0, 0)),
                pl.BlockSpec((2, 4, share_len), lambda i, b: (0, 0, b[0])),
                pl.BlockSpec((1, share_len), lambda i, b: (0, b[0])),
                pl.BlockSpec((2, share_len), lambda i, b: (0, b[0])),
            ],
            out_specs=(
                pl.BlockSpec((2, 4, share_len), lambda i, b: (0, 0, 0)),
                pl.BlockSpec((2, 4, share_len), lambda i, b: (0, 0, 0)),
            ),
        ),
        out_shape=(
            jax.ShapeDtypeStruct((2, 4, share_len), F32),
            jax.ShapeDtypeStruct((2, 4, share_len), F32),
        ),
        compiler_params=params,
        name="update",
    )(band, parts, right_side, beam_row, inv_spectra)


def solution(mesh):
    placed = (
        P("harm", None, None),
        P(),
        P(),
        P("harm"),
        P("harm", None, None, "band"),
        P(None, "harm", "band", None, None),
        P(None, "harm", "band", None, None),
        P(None, "harm", "band", None, None),
        P("harm", "band", None),
    )
    return jax.shard_map(
        local,
        mesh=mesh,
        in_specs=placed,
        out_specs=(P("harm", None, "band"), P("harm", None, "band")),
        check_vma=False,
    )
```

```python
import functools
import math

import jax
import jax.numpy as jnp
from jax import lax
from jax.experimental import pallas as pl
from jax.experimental.pallas import tpu as pltpu
from jax.sharding import PartitionSpec as P

NPHI = 20480
ROWS = 144
LANES = 256
PIECE = 640
BLOCK = 256
VMEM_LIMIT = 16 * 1024 * 1024
AHEAD = 4
PARTS = 2
STREAM_LIMIT = 46 * 1024 * 1024
F32 = jnp.float32
BF16 = jnp.bfloat16


def split3(value):
    first = value.astype(BF16).astype(F32)
    rest = value - first
    second = rest.astype(BF16).astype(F32)
    third = (rest - second).astype(BF16).astype(F32)
    return first, second, third


def trig_tables(modes):
    lane = lax.broadcasted_iota(jnp.int32, (64, 128), 1)
    digit = lane & 31
    steps = jnp.where(
        lane < 32, digit * 1024, jnp.where(lane < 64, digit * 32, jnp.where(lane < 96, digit, lane & 3))
    )
    product = modes * steps
    high = product >> 12
    turn = (high - 5 * ((high * 52429) >> 18)) * 4096 + (product & 4095)
    quarter = jnp.zeros_like(turn)
    for edge in (2560, 7680, 12800, 17920):
        quarter = quarter + (turn >= edge).astype(jnp.int32)
    angle = (turn - 5120 * quarter).astype(F32) * (2.0 * math.pi / NPHI)
    quarter = quarter & 3
    sq = angle * angle
    sine = angle * (1.0 + sq * (-1.0 / 6 + sq * (1.0 / 120 + sq * (-1.0 / 5040 + sq * (1.0 / 362880)))))
    cosine = 1.0 + sq * (
        -0.5 + sq * (1.0 / 24 + sq * (-1.0 / 720 + sq * (1.0 / 40320 - sq * (1.0 / 3628800))))
    )
    cos_out = jnp.where(
        quarter == 0, cosine, jnp.where(quarter == 1, -sine, jnp.where(quarter == 2, -cosine, sine))
    )
    sin_out = jnp.where(
        quarter == 0, sine, jnp.where(quarter == 1, cosine, jnp.where(quarter == 2, -sine, -cosine))
    )
    return cos_out, sin_out


def pack_kernel(
    band_ref, counts_ref, weights_ref, base_ref, noise_ref, side_ref, beam_ref, spectra_ref,
    data_ref, blocks_ref, share_ref,
):
    data_ref[...] = jnp.zeros_like(data_ref)
    lane = lax.broadcasted_iota(jnp.int32, (24, 128), 1)
    used = jnp.int32(0)
    for owner in range(32):
        count = counts_ref[0, 0, owner]
        pixel = base_ref[1, owner : owner + 1, :] + (owner * 640 - 2)
        if owner == 0:
            pixel = jnp.where(pixel < 0, pixel + NPHI, pixel)
        if owner == 31:
            pixel = jnp.where(pixel >= NPHI, pixel - NPHI, pixel)
        live = jnp.concatenate(
            [
                weights_ref[:, owner, :],
                base_ref[0, owner : owner + 1, :].astype(F32),
                pixel.astype(F32),
                noise_ref[:, owner, :],
                jnp.zeros((4, 128), F32),
            ],
            axis=0,
        )
        live = jnp.where(lane < count, live, 0.0)
        shift = used & 127
        live = pltpu.roll(live, shift, 1)
        start = pl.multiple_of((used >> 7) * 128, 128)
        here = data_ref[:, pl.ds(start, 128)]
        data_ref[:, pl.ds(start, 128)] = jnp.where(lane >= shift, live, here)
        after = pl.multiple_of(start + 128, 128)
        data_ref[:, pl.ds(after, 128)] = jnp.where(lane < shift, live, 0.0)
        used = used + count
    blocks_ref[...] = jnp.full(blocks_ref.shape, (used + (BLOCK - 1)) // BLOCK, jnp.int32)
    length = share_ref.shape[1]
    place = pl.ds(pl.multiple_of(band_ref[0] * length, 128), length)
    share_ref[0:4] = side_ref[0, :, place]
    share_ref[4:8] = side_ref[1, :, place]
    share_ref[8:9] = beam_ref[:, place]
    share_ref[9:11] = spectra_ref[:, place]
    share_ref[11:16] = jnp.zeros((5, length), F32)


def to_pieces(low, high, extra, first, count):
    lane = lax.broadcasted_iota(jnp.int32, low[0].shape, 1)
    rest = jnp.where((lane >= 16) & (lane < 16 + count), pltpu.roll(extra, 16 - first, 1), 0.0)
    for q in range(4):
        moved = pltpu.roll(high[q], 4 * q, 1) if q else high[q]
        rest = jnp.where((lane >= 4 * q) & (lane < 4 * q + 4), moved, rest)
    return jnp.concatenate(low + [rest], axis=1)


def points_kernel(
    blocks_ref, sums_ref, x_ref, data_ref, source_ref, out_ref, legendre_ref, table_ref, field_ref, acc_ref, curv_ref, grid_ref, wave_ref, term_ref, hit_ref, sem
):
    move = pltpu.make_async_copy(source_ref, legendre_ref, sem)
    move.start()
    got = jnp.concatenate([x_ref[source].astype(F32) for source in range(32)], axis=0)
    rest = got[:, 512:640]
    lane = lax.broadcasted_iota(jnp.int32, (64, 128), 1)
    for q in range(4):
        rows = slice(64 * q, 64 * q + 64)
        field_ref[rows, 0:128] = got[:, 128 * q : 128 * q + 128].astype(BF16)
        moved = pltpu.roll(rest, 128 - 4 * q, 1) if q else rest
        field_ref[rows, 128:256] = jnp.where(lane < 4, moved, 0.0).astype(BF16)
    grid_ref[...] = lax.broadcasted_iota(jnp.int32, (ROWS, BLOCK), 0).astype(F32).astype(BF16)
    mode_value = jnp.sum(
        jnp.where(lane == 16, rest * 64.0, jnp.where(lane == 17, rest, 0.0)), axis=1, keepdims=True
    )
    modes = jnp.broadcast_to(mode_value, (64, 128)).astype(jnp.int32)
    cos_tab, sin_tab = trig_tables(modes)
    weight = jnp.where(modes == 0, 1.0, 2.0).astype(F32) * 128.0**-0.5
    groups = [
        (lane < 32, weight),
        ((lane >= 32) & (lane < 64), None),
        ((lane >= 64) & (lane < 96), None),
    ]
    for a in range(4):
        groups.append(((lane >= 96) & (((lane - 96) & 15) >> 2 == a), None))
    for index, (mask, gain) in enumerate(groups):
        for part, table in enumerate((cos_tab, -sin_tab)):
            value = table if gain is None else table * gain
            value = jnp.where(mask, value, 0.0)
            rounded = value.astype(BF16)
            start = (2 * index + part) * 64
            table_ref[pl.ds(start, 64), 0:128] = rounded
            table_ref[pl.ds(start, 64), 128:256] = (value - rounded.astype(F32)).astype(BF16)
    acc_ref[...] = jnp.zeros_like(acc_ref)
    curv_ref[...] = jnp.zeros_like(curv_ref)
    one = jnp.ones((), BF16)
    zero = jnp.zeros((), BF16)

    term_ref[...] = jnp.zeros_like(term_ref)
    hit_ref[...] = jnp.zeros_like(hit_ref)

    def spread():
        acc_ref[:, 0:ROWS] += lax.dot_general(
            term_ref[...], hit_ref[...], (((1,), (1,)), ((), ())), preferred_element_type=F32
        )

    def sample(index):
        start = pl.multiple_of(index * BLOCK, BLOCK)
        info = data_ref[16:24, pl.ds(start, BLOCK)]
        first_row = info[0:1]
        grid_row = grid_ref[...]
        total = [None, None]
        for a in range(4):
            row_hit = jnp.where(grid_row == (first_row + float(a)).astype(BF16), one, zero)
            hit_ref[:, a * BLOCK : (a + 1) * BLOCK] = row_hit
            picked = jnp.dot(field_ref[:, 0:ROWS], row_hit, preferred_element_type=F32)
            wave_re = wave_ref[2 * a]
            wave_im = wave_ref[2 * a + 1]
            for f in range(2):
                term = (
                    picked[128 * f : 128 * f + 64] * wave_re
                    + picked[128 * f + 64 : 128 * f + 128] * wave_im
                )
                total[f] = term if a == 0 else total[f] + term
        weighted = []
        for f in range(2):
            sampled = jnp.sum(total[f], axis=0, keepdims=True)
            value = info[2 + f : 3 + f] * sampled
            curv_ref[f : f + 1, :] += value * sampled
            weighted.append(value)
        for a in range(4):
            for f in range(2):
                for part in range(2):
                    row = 128 * f + 64 * part
                    term_ref[row : row + 64, a * BLOCK : (a + 1) * BLOCK] = (
                        weighted[f] * wave_ref[2 * a + part]
                    ).astype(BF16)

    def turn(index):
        data = data_ref[:, pl.ds(pl.multiple_of(index * BLOCK, BLOCK), BLOCK)]
        pixel = data[17:18].astype(jnp.int32)
        digit_id = grid_ref[0:32, :]
        hit = [
            jnp.where(digit_id == digit.astype(F32).astype(BF16), one, zero)
            for digit in (pixel >> 10, (pixel >> 5) & 31, pixel & 31)
        ]
        weights = data[0:16]
        weights_high = weights.astype(BF16)
        weights_low = (weights - weights_high.astype(F32)).astype(BF16)
        chosen = jnp.concatenate(hit + [weights_high, weights_low], axis=0)
        phases = jnp.dot(
            table_ref[...], jnp.concatenate([chosen, chosen], axis=0), preferred_element_type=F32
        )
        part = [phases[64 * i : 64 * (i + 1)] for i in range(14)]
        mid_re = part[0] * part[2] - part[1] * part[3]
        mid_im = part[0] * part[3] + part[1] * part[2]
        turn_re = mid_re * part[4] - mid_im * part[5]
        turn_im = mid_re * part[5] + mid_im * part[4]
        for a in range(4):
            wave_ref[2 * a] = turn_re * part[6 + 2 * a] - turn_im * part[7 + 2 * a]
            wave_ref[2 * a + 1] = turn_re * part[7 + 2 * a] + turn_im * part[6 + 2 * a]

    def block_step(index, carry):
        spread()
        sample(index)
        turn(index + 1)
        return carry

    turn(0)
    lax.fori_loop(0, jnp.max(blocks_ref[...]), block_step, 0)
    spread()
    curvature = jnp.sum(curv_ref[...], axis=(0, 1), keepdims=True) + jnp.sum(
        sums_ref[8:16], axis=(0, 1), keepdims=True
    )
    norm = jnp.sum(sums_ref[0:8], axis=(0, 1), keepdims=True)
    extra = jnp.zeros((64, 128), F32)
    for offset, piece in enumerate(split3(curvature) + split3(norm)):
        extra = jnp.where(lane == offset, piece, extra)
    back = [acc_ref[64 * q : 64 * q + 64] for q in range(4)]
    sent = to_pieces([b[:, 0:128] for b in back], [b[:, 128:256] for b in back], extra, 0, 6)
    for target in range(32):
        out_ref[target] = sent[2 * target : 2 * target + 2].astype(BF16)
    move.wait()


def swap_rows(value):
    return jnp.concatenate(
        [
            value[3:4],
            -value[2:3],
            -value[1:2],
            value[0:1],
            value[7:8],
            -value[6:7],
            -value[5:6],
            value[4:5],
        ],
        axis=0,
    )


def scaled_rows(side_ref, beam_ref):
    rows = jnp.concatenate([side_ref[0], side_ref[1]], axis=0)
    return rows, (rows * beam_ref[...]).astype(BF16)


def fetch(source_ref, target_ref, sems, part, m, t):
    chunk = source_ref.shape[2] // sems.shape[0]
    place = pl.ds(part * chunk, chunk)
    return pltpu.make_async_copy(
        source_ref.at[m, t, place], target_ref.at[m, t, place], sems.at[part, m, t]
    )


def start_fetch(source_ref, target_ref, sems, part):
    if part < sems.shape[0]:
        for m in range(2):
            for t in range(2):
                fetch(source_ref, target_ref, sems, part, m, t).start()


def next_part(source_ref, target_ref, sems, part):
    for m in range(2):
        for t in range(2):
            fetch(source_ref, target_ref, sems, part, m, t).wait()
    start_fetch(source_ref, target_ref, sems, part + AHEAD)


def edge_kernel(source_ref, low_ref, high_ref, legendre_ref, sems):
    parts = sems.shape[0]
    chunk = source_ref.shape[2] // parts
    for part in range(AHEAD):
        start_fetch(source_ref, legendre_ref, sems, part)
    row = lax.broadcasted_iota(jnp.int32, (16, 256), 0)
    lane = lax.broadcasted_iota(jnp.int32, (16, 256), 1)
    cycle = (row & 1) + jnp.where(row >= 8, 126, 0)
    picks = []
    for m in range(2):
        pick = (((row >> 1) & 3) == 2 * m + (lane >> 7)) & ((lane & 127) == cycle)
        picks.append(pick.astype(F32).astype(BF16))
    for part in range(parts):
        place = slice(part * chunk, (part + 1) * chunk)
        edges = jnp.zeros((16, chunk), F32)
        next_part(source_ref, legendre_ref, sems, part)
        for m in range(2):
            table = jnp.concatenate([legendre_ref[m, 0, place], legendre_ref[m, 1, place]], axis=1)
            edges = edges + lax.dot_general(
                picks[m], table, (((1,), (1,)), ((), ())), preferred_element_type=F32
            )
        high_ref[:, place] = edges[0:8].astype(BF16)
        low_ref[:, place] = edges[8:16].astype(BF16)


def synth_kernel(
    m_ref, side_ref, beam_ref, spectra_ref, legendre_ref, own_ref, coef_ref, sums_ref
):
    rows, coef = scaled_rows(side_ref, beam_ref)
    square = rows * rows
    spectra = spectra_ref[...]
    pair = jnp.concatenate([spectra[0:1]] * 2 + [spectra[1:2]] * 2, axis=0)
    prior = square * jnp.concatenate([pair, pair], axis=0)
    norm_sum = square[:, 0:128]
    prior_sum = prior[:, 0:128]
    for start in range(128, rows.shape[1], 128):
        norm_sum = norm_sum + square[:, start : start + 128]
        prior_sum = prior_sum + prior[:, start : start + 128]
    sums_ref[...] = jnp.concatenate([norm_sum, prior_sum], axis=0) * 0.125
    own = []
    for m in range(2):
        table = jnp.concatenate([legendre_ref[m, 0], legendre_ref[m, 1]], axis=1)
        own.append(jnp.dot(coef, table, preferred_element_type=F32)[4 * m : 4 * m + 4])
    modes = jnp.concatenate(own, axis=0)
    fields = pltpu.roll(swap_rows(modes[:, 128:256]) - modes[:, 0:128], 2, 1)
    row = lax.broadcasted_iota(jnp.int32, (8, 128), 0)
    lane = lax.broadcasted_iota(jnp.int32, (8, 128), 1)
    own_ref[0:8] = jnp.where(lane < 2, 0.0, fields)
    mode = jnp.where(row < 4, m_ref[:, 0:1], m_ref[:, 1:2])
    high = jnp.where(lane < 2, fields, 0.0)
    high = jnp.where(lane == 4, (mode >> 6).astype(F32), high)
    own_ref[8:16] = jnp.where(lane == 5, (mode & 63).astype(F32), high)
    coef_ref[...] = coef


def both_modes(value, q):
    return jnp.concatenate([value[q : q + 1], value[q + 4 : q + 5]], axis=0)


def fields_kernel(coef_ref, low_ref, high_ref, own_ref, out_ref):
    rims = jnp.concatenate([low_ref[...], high_ref[...]], axis=0)
    rim = lax.dot_general(
        coef_ref[...], rims, (((1,), (1,)), ((), ())), preferred_element_type=F32
    )
    rim = jnp.concatenate([rim, jnp.zeros((8, 112), F32)], axis=1)
    row = lax.broadcasted_iota(jnp.int32, (8, 128), 0)
    lane = lax.broadcasted_iota(jnp.int32, (8, 128), 1)
    rim = jnp.where(row < 4, rim, pltpu.roll(rim, 124, 1))
    rim = swap_rows(pltpu.roll(rim, 126, 1)) - rim
    low = jnp.where(lane < 2, rim, own_ref[0:8])
    high = jnp.where((lane == 2) | (lane == 3), pltpu.roll(rim, 122, 1), own_ref[8:16])
    sent = to_pieces([both_modes(low, q) for q in range(4)], [both_modes(high, q) for q in range(4)], both_modes(high, 0), 4, 2)
    sent = sent.astype(BF16)
    for target in range(32):
        out_ref[target] = sent


def analysis_kernel(got_ref, low_ref, high_ref, legendre_ref, out_ref):
    total = got_ref[0].astype(F32)
    for source in range(1, 32):
        total = total + got_ref[source].astype(F32)
    lane = lax.broadcasted_iota(jnp.int32, (8, 128), 1)
    row = lax.broadcasted_iota(jnp.int32, (8, 128), 0)
    rest = total[:, 512:640]
    low = jnp.concatenate(
        [total[m : m + 1, 128 * q : 128 * q + 128] for m in range(2) for q in range(4)], axis=0
    )
    moved = [pltpu.roll(rest, 128 - 4 * q, 1) if q else rest for q in range(4)]
    high = jnp.concatenate([moved[q][m : m + 1] for m in range(2) for q in range(4)], axis=0)
    extra = jnp.broadcast_to(rest[0:1], (8, 128))
    curvature = jnp.sum(
        jnp.where((lane >= 16) & (lane < 19), extra, 0.0), axis=1, keepdims=True
    )
    norm = jnp.sum(jnp.where((lane >= 19) & (lane < 22), extra, 0.0), axis=1, keepdims=True)
    sums = jnp.where(lane == 0, curvature, jnp.where(lane == 1, norm, 0.0))
    own = jnp.where(lane < 126, pltpu.roll(low, 126, 1), pltpu.roll(high, 126, 1))
    own_both = jnp.concatenate([-own, swap_rows(own)], axis=1)
    row_both = lax.broadcasted_iota(jnp.int32, (8, 256), 0)
    owns = []
    for m in range(2):
        owns.append(jnp.where((row_both >> 2) == m, own_both, 0.0).astype(BF16))
    low_swap, high_swap = swap_rows(low), swap_rows(high)
    rim = jnp.where(lane < 2, -low, jnp.where(lane < 4, pltpu.roll(low_swap, 2, 1), 0.0))
    rim = jnp.where((lane >= 8) & (lane < 10), pltpu.roll(-high, 6, 1), rim)
    rim = jnp.where((lane >= 10) & (lane < 12), pltpu.roll(high_swap, 8, 1), rim)
    rim = jnp.where(row < 4, rim, pltpu.roll(rim, 4, 1)).astype(BF16)


    bands = out_ref.shape[0]
    chunk = legendre_ref.shape[2] // bands
    for band in range(bands):
        place = slice(band * chunk, (band + 1) * chunk)
        rims = jnp.concatenate([low_ref[:, place], high_ref[:, place]], axis=0)
        result = jnp.dot(rim[:, 0:16], rims, preferred_element_type=F32)
        for m in range(2):
            table = jnp.concatenate([legendre_ref[m, 0, place], legendre_ref[m, 1, place]], axis=1)
            result = result + lax.dot_general(
                owns[m], table, (((1,), (1,)), ((), ())), preferred_element_type=F32
            )
        out_ref[band, :, 0:chunk] = result
        out_ref[band, :, chunk : chunk + 128] = sums


def update_kernel(parts_ref, share_ref, solution_ref, residual_ref):
    total = parts_ref[0]
    for source in range(1, parts_ref.shape[0]):
        total = total + parts_ref[source]
    length = share_ref.shape[1]
    step = total[0:1, length + 1 : length + 2] / total[0:1, length : length + 1]
    beam = share_ref[8:9]
    spectra = share_ref[9:11]
    pair = jnp.concatenate([spectra[0:1]] * 2 + [spectra[1:2]] * 2, axis=0)
    for m in range(2):
        side = share_ref[4 * m : 4 * m + 4]
        image = pair * side + beam * total[4 * m : 4 * m + 4, 0:length]
        solution_ref[m] = step * side
        residual_ref[m] = side - step * image


def local(
    right_side,
    inv_spectra,
    beam,
    m_values,
    legendre,
    stencil_weights,
    stencil_base,
    inv_noise,
    slot_counts,
):
    band_count = lax.axis_size("band")
    lmax_len = right_side.shape[2]
    share_len = lmax_len // band_count
    smem = pl.BlockSpec(memory_space=pltpu.SMEM)
    vmem = pl.BlockSpec(memory_space=pltpu.VMEM)
    params = pltpu.CompilerParams(vmem_limit_bytes=VMEM_LIMIT)
    stream_params = pltpu.CompilerParams(vmem_limit_bytes=STREAM_LIMIT)
    hbm = pl.BlockSpec(memory_space=pl.ANY)
    beam_row = beam.reshape(1, lmax_len)

    low_edge, high_edge, near_table = pl.pallas_call(
        edge_kernel,
        out_shape=(
            jax.ShapeDtypeStruct((8, lmax_len), BF16),
            jax.ShapeDtypeStruct((8, lmax_len), BF16),
            jax.ShapeDtypeStruct(legendre.shape, BF16),
        ),
        in_specs=[hbm],
        out_specs=(vmem, vmem, vmem),
        scratch_shapes=[pltpu.SemaphoreType.DMA((PARTS, 2, 2))],
        compiler_params=stream_params,
        name="edges",
    )(legendre)
    own_fields, coef, sums = pl.pallas_call(
        synth_kernel,
        out_shape=(
            jax.ShapeDtypeStruct((16, 128), F32),
            jax.ShapeDtypeStruct((8, lmax_len), BF16),
            jax.ShapeDtypeStruct((16, 128), F32),
        ),
        in_specs=[vmem] * 5,
        out_specs=(vmem, vmem, vmem),
        compiler_params=params,
        cost_estimate=pl.CostEstimate(flops=10**7, bytes_accessed=6 * 10**6, transcendentals=0),
        name="synth",
    )(m_values.reshape(1, 2), right_side, beam_row, inv_spectra, near_table)
    up = [(i, i + 1) for i in range(band_count - 1)]
    down = [(i + 1, i) for i in range(band_count - 1)]
    low_rim = lax.ppermute(low_edge, "band", up)
    high_rim = lax.ppermute(high_edge, "band", down)

    band = lax.axis_index("band").astype(jnp.int32).reshape(1)
    data, blocks, share = pl.pallas_call(
        pack_kernel,
        out_shape=(
            jax.ShapeDtypeStruct((24, 4096 + 128 + 3 * BLOCK), F32),
            jax.ShapeDtypeStruct((8, 128), jnp.int32),
            jax.ShapeDtypeStruct((16, share_len), F32),
        ),
        in_specs=[smem, smem] + [vmem] * 6,
        out_specs=(vmem, vmem, vmem),
        compiler_params=params,
        cost_estimate=pl.CostEstimate(flops=10**6, bytes_accessed=3 * 10**6, transcendentals=0),
        name="pack",
    )(
        band,
        slot_counts,
        stencil_weights.reshape(16, 32, 128),
        stencil_base.reshape(2, 32, 128),
        inv_noise.reshape(2, 32, 128),
        right_side,
        beam_row,
        inv_spectra,
    )

    sent = pl.pallas_call(
        fields_kernel,
        out_shape=jax.ShapeDtypeStruct((32, 2, PIECE), BF16),
        in_specs=[vmem, vmem, vmem, vmem],
        out_specs=vmem,
        compiler_params=params,
        name="fields",
    )(coef, low_rim, high_rim, own_fields)
    got = lax.all_to_all(sent, "harm", split_axis=0, concat_axis=0, tiled=True)

    back, table = pl.pallas_call(
        points_kernel,
        out_shape=(
            jax.ShapeDtypeStruct((32, 2, PIECE), BF16),
            jax.ShapeDtypeStruct(legendre.shape, BF16),
        ),
        in_specs=[vmem, vmem, vmem, vmem, hbm],
        out_specs=(vmem, vmem),
        scratch_shapes=[
            pltpu.VMEM((896, 256), BF16),
            pltpu.VMEM((256, LANES), BF16),
            pltpu.VMEM((256, LANES), F32),
            pltpu.VMEM((2, BLOCK), F32),
            pltpu.VMEM((ROWS, BLOCK), BF16),
            pltpu.VMEM((8, 64, BLOCK), F32),
            pltpu.VMEM((256, 4 * BLOCK), BF16),
            pltpu.VMEM((ROWS, 4 * BLOCK), BF16),
            pltpu.SemaphoreType.DMA(()),
        ],
        compiler_params=stream_params,
        name="points",
    )(blocks, sums, got, data, legendre)
    back_got = lax.all_to_all(back, "harm", split_axis=0, concat_axis=0, tiled=True)

    harmonic = pl.pallas_call(
        analysis_kernel,
        out_shape=jax.ShapeDtypeStruct((band_count, 8, share_len + 128), F32),
        in_specs=[vmem, vmem, vmem, vmem],
        out_specs=vmem,
        compiler_params=params,
        name="analysis",
    )(back_got, low_rim, high_rim, table)
    parts = lax.all_to_all(harmonic, "band", split_axis=0, concat_axis=0, tiled=True)

    return pl.pallas_call(
        update_kernel,
        out_shape=(
            jax.ShapeDtypeStruct((2, 4, share_len), F32),
            jax.ShapeDtypeStruct((2, 4, share_len), F32),
        ),
        in_specs=[vmem, vmem],
        out_specs=(vmem, vmem),
        compiler_params=params,
        name="update",
    )(parts, share)


def solution(mesh):
    placed = (
        P("harm", None, None),
        P(),
        P(),
        P("harm"),
        P("harm", None, None, "band"),
        P(None, "harm", "band", None, None),
        P(None, "harm", "band", None, None),
        P(None, "harm", "band", None, None),
        P("harm", "band", None),
    )
    return jax.shard_map(
        local,
        mesh=mesh,
        in_specs=placed,
        out_specs=(P("harm", None, "band"), P("harm", None, "band")),
        check_vma=False,
    )
```

```python
import functools
import math

import jax
import jax.numpy as jnp
from jax import lax
from jax.experimental import pallas as pl
from jax.experimental.pallas import tpu as pltpu
from jax.sharding import PartitionSpec as P

NPHI = 20480
ROWS = 144
LANES = 256
PIECE = 640
BLOCK = 256
VMEM_LIMIT = 16 * 1024 * 1024
AHEAD = 4
PARTS = 2
STREAM_LIMIT = 46 * 1024 * 1024
F32 = jnp.float32
BF16 = jnp.bfloat16


def split3(value):
    first = value.astype(BF16).astype(F32)
    rest = value - first
    second = rest.astype(BF16).astype(F32)
    third = (rest - second).astype(BF16).astype(F32)
    return first, second, third


def trig_tables(modes):
    lane = lax.broadcasted_iota(jnp.int32, (64, 128), 1)
    digit = lane & 31
    steps = jnp.where(
        lane < 32, digit * 1024, jnp.where(lane < 64, digit * 32, jnp.where(lane < 96, digit, lane & 3))
    )
    product = modes * steps
    high = product >> 12
    turn = (high - 5 * ((high * 52429) >> 18)) * 4096 + (product & 4095)
    quarter = jnp.zeros_like(turn)
    for edge in (2560, 7680, 12800, 17920):
        quarter = quarter + (turn >= edge).astype(jnp.int32)
    angle = (turn - 5120 * quarter).astype(F32) * (2.0 * math.pi / NPHI)
    quarter = quarter & 3
    sq = angle * angle
    sine = angle * (1.0 + sq * (-1.0 / 6 + sq * (1.0 / 120 + sq * (-1.0 / 5040 + sq * (1.0 / 362880)))))
    cosine = 1.0 + sq * (
        -0.5 + sq * (1.0 / 24 + sq * (-1.0 / 720 + sq * (1.0 / 40320 - sq * (1.0 / 3628800))))
    )
    cos_out = jnp.where(
        quarter == 0, cosine, jnp.where(quarter == 1, -sine, jnp.where(quarter == 2, -cosine, sine))
    )
    sin_out = jnp.where(
        quarter == 0, sine, jnp.where(quarter == 1, cosine, jnp.where(quarter == 2, -sine, -cosine))
    )
    return cos_out, sin_out


def pack_kernel(
    band_ref, counts_ref, weights_ref, base_ref, noise_ref, side_ref, beam_ref, spectra_ref,
    data_ref, blocks_ref, share_ref,
):
    data_ref[...] = jnp.zeros_like(data_ref)
    lane = lax.broadcasted_iota(jnp.int32, (24, 128), 1)
    used = jnp.int32(0)
    for owner in range(32):
        count = counts_ref[0, 0, owner]
        pixel = base_ref[1, owner : owner + 1, :] + (owner * 640 - 2)
        if owner == 0:
            pixel = jnp.where(pixel < 0, pixel + NPHI, pixel)
        if owner == 31:
            pixel = jnp.where(pixel >= NPHI, pixel - NPHI, pixel)
        live = jnp.concatenate(
            [
                weights_ref[:, owner, :],
                base_ref[0, owner : owner + 1, :].astype(F32),
                pixel.astype(F32),
                noise_ref[:, owner, :],
                jnp.zeros((4, 128), F32),
            ],
            axis=0,
        )
        live = jnp.where(lane < count, live, 0.0)
        shift = used & 127
        live = pltpu.roll(live, shift, 1)
        start = pl.multiple_of((used >> 7) * 128, 128)
        here = data_ref[:, pl.ds(start, 128)]
        data_ref[:, pl.ds(start, 128)] = jnp.where(lane >= shift, live, here)
        after = pl.multiple_of(start + 128, 128)
        data_ref[:, pl.ds(after, 128)] = jnp.where(lane < shift, live, 0.0)
        used = used + count
    blocks_ref[...] = jnp.full(blocks_ref.shape, (used + (BLOCK - 1)) // BLOCK, jnp.int32)
    length = share_ref.shape[1]
    place = pl.ds(pl.multiple_of(band_ref[0] * length, 128), length)
    share_ref[0:4] = side_ref[0, :, place]
    share_ref[4:8] = side_ref[1, :, place]
    share_ref[8:9] = beam_ref[:, place]
    share_ref[9:11] = spectra_ref[:, place]
    share_ref[11:16] = jnp.zeros((5, length), F32)


def to_pieces(low, high, extra, first, count):
    lane = lax.broadcasted_iota(jnp.int32, low[0].shape, 1)
    rest = jnp.where((lane >= 16) & (lane < 16 + count), pltpu.roll(extra, 16 - first, 1), 0.0)
    for q in range(4):
        moved = pltpu.roll(high[q], 4 * q, 1) if q else high[q]
        rest = jnp.where((lane >= 4 * q) & (lane < 4 * q + 4), moved, rest)
    return jnp.concatenate(low + [rest], axis=1)


def points_kernel(
    blocks_ref, sums_ref, x_ref, data_ref, source_ref, out_ref, legendre_ref, table_ref, field_ref, acc_ref, curv_ref, grid_ref, wave_ref, term_ref, hit_ref, sem
):
    move = pltpu.make_async_copy(source_ref, legendre_ref, sem)
    move.start()
    got = jnp.concatenate([x_ref[source].astype(F32) for source in range(32)], axis=0)
    rest = got[:, 512:640]
    lane = lax.broadcasted_iota(jnp.int32, (64, 128), 1)
    for q in range(4):
        rows = slice(64 * q, 64 * q + 64)
        field_ref[rows, 0:128] = got[:, 128 * q : 128 * q + 128].astype(BF16)
        moved = pltpu.roll(rest, 128 - 4 * q, 1) if q else rest
        field_ref[rows, 128:256] = jnp.where(lane < 4, moved, 0.0).astype(BF16)
    grid_ref[...] = lax.broadcasted_iota(jnp.int32, (ROWS, BLOCK), 0).astype(F32).astype(BF16)
    mode_value = jnp.sum(
        jnp.where(lane == 16, rest * 64.0, jnp.where(lane == 17, rest, 0.0)), axis=1, keepdims=True
    )
    modes = jnp.broadcast_to(mode_value, (64, 128)).astype(jnp.int32)
    cos_tab, sin_tab = trig_tables(modes)
    weight = jnp.where(modes == 0, 1.0, 2.0).astype(F32) * 128.0**-0.5
    groups = [
        (lane < 32, weight),
        ((lane >= 32) & (lane < 64), None),
        ((lane >= 64) & (lane < 96), None),
    ]
    for a in range(4):
        groups.append(((lane >= 96) & (((lane - 96) & 15) >> 2 == a), None))
    for index, (mask, gain) in enumerate(groups):
        for part, table in enumerate((cos_tab, -sin_tab)):
            value = table if gain is None else table * gain
            value = jnp.where(mask, value, 0.0)
            rounded = value.astype(BF16)
            start = (2 * index + part) * 64
            table_ref[pl.ds(start, 64), 0:128] = rounded
            table_ref[pl.ds(start, 64), 128:256] = (value - rounded.astype(F32)).astype(BF16)
    acc_ref[...] = jnp.zeros_like(acc_ref)
    curv_ref[...] = jnp.zeros_like(curv_ref)
    one = jnp.ones((), BF16)
    zero = jnp.zeros((), BF16)

    term_ref[...] = jnp.zeros_like(term_ref)
    hit_ref[...] = jnp.zeros_like(hit_ref)

    def spread():
        acc_ref[:, 0:ROWS] += lax.dot_general(
            term_ref[...], hit_ref[...], (((1,), (1,)), ((), ())), preferred_element_type=F32
        )

    def sample(index):
        start = pl.multiple_of(index * BLOCK, BLOCK)
        info = data_ref[16:24, pl.ds(start, BLOCK)]
        first_row = info[0:1]
        grid_row = grid_ref[...]
        total = [None, None]
        for a in range(4):
            row_hit = jnp.where(grid_row == (first_row + float(a)).astype(BF16), one, zero)
            hit_ref[:, a * BLOCK : (a + 1) * BLOCK] = row_hit
            picked = jnp.dot(field_ref[:, 0:ROWS], row_hit, preferred_element_type=F32)
            wave_re = wave_ref[2 * a]
            wave_im = wave_ref[2 * a + 1]
            for f in range(2):
                term = (
                    picked[128 * f : 128 * f + 64] * wave_re
                    + picked[128 * f + 64 : 128 * f + 128] * wave_im
                )
                total[f] = term if a == 0 else total[f] + term
        weighted = []
        for f in range(2):
            sampled = jnp.sum(total[f], axis=0, keepdims=True)
            value = info[2 + f : 3 + f] * sampled
            curv_ref[f : f + 1, :] += value * sampled
            weighted.append(value)
        for a in range(4):
            for f in range(2):
                for part in range(2):
                    row = 128 * f + 64 * part
                    term_ref[row : row + 64, a * BLOCK : (a + 1) * BLOCK] = (
                        weighted[f] * wave_ref[2 * a + part]
                    ).astype(BF16)

    def turn(index):
        data = data_ref[:, pl.ds(pl.multiple_of(index * BLOCK, BLOCK), BLOCK)]
        pixel = data[17:18].astype(jnp.int32)
        digit_id = grid_ref[0:32, :]
        hit = [
            jnp.where(digit_id == digit.astype(F32).astype(BF16), one, zero)
            for digit in (pixel >> 10, (pixel >> 5) & 31, pixel & 31)
        ]
        weights = data[0:16]
        weights_high = weights.astype(BF16)
        weights_low = (weights - weights_high.astype(F32)).astype(BF16)
        chosen = jnp.concatenate(hit + [weights_high, weights_low], axis=0)
        phases = jnp.dot(
            table_ref[...], jnp.concatenate([chosen, chosen], axis=0), preferred_element_type=F32
        )
        part = [phases[64 * i : 64 * (i + 1)] for i in range(14)]
        mid_re = part[0] * part[2] - part[1] * part[3]
        mid_im = part[0] * part[3] + part[1] * part[2]
        turn_re = mid_re * part[4] - mid_im * part[5]
        turn_im = mid_re * part[5] + mid_im * part[4]
        for a in range(4):
            wave_ref[2 * a] = turn_re * part[6 + 2 * a] - turn_im * part[7 + 2 * a]
            wave_ref[2 * a + 1] = turn_re * part[7 + 2 * a] + turn_im * part[6 + 2 * a]

    def block_step(index, carry):
        spread()
        sample(index)
        turn(index + 1)
        return carry

    turn(0)
    lax.fori_loop(0, jnp.max(blocks_ref[...]), block_step, 0)
    spread()
    curvature = jnp.sum(curv_ref[...], axis=(0, 1), keepdims=True) + jnp.sum(
        sums_ref[8:16], axis=(0, 1), keepdims=True
    )
    norm = jnp.sum(sums_ref[0:8], axis=(0, 1), keepdims=True)
    extra = jnp.zeros((64, 128), F32)
    for offset, piece in enumerate(split3(curvature) + split3(norm)):
        extra = jnp.where(lane == offset, piece, extra)
    back = [acc_ref[64 * q : 64 * q + 64] for q in range(4)]
    sent = to_pieces([b[:, 0:128] for b in back], [b[:, 128:256] for b in back], extra, 0, 6)
    for target in range(32):
        out_ref[target] = sent[2 * target : 2 * target + 2].astype(BF16)
    move.wait()


def swap_rows(value):
    return jnp.concatenate(
        [
            value[3:4],
            -value[2:3],
            -value[1:2],
            value[0:1],
            value[7:8],
            -value[6:7],
            -value[5:6],
            value[4:5],
        ],
        axis=0,
    )


def scaled_rows(side_ref, beam_ref):
    rows = jnp.concatenate([side_ref[0], side_ref[1]], axis=0)
    return rows, (rows * beam_ref[...]).astype(BF16)


def fetch(source_ref, target_ref, sems, part, m, t):
    chunk = source_ref.shape[2] // sems.shape[0]
    place = pl.ds(part * chunk, chunk)
    return pltpu.make_async_copy(
        source_ref.at[m, t, place], target_ref.at[m, t, place], sems.at[part, m, t]
    )


def start_fetch(source_ref, target_ref, sems, part):
    if part < sems.shape[0]:
        for m in range(2):
            for t in range(2):
                fetch(source_ref, target_ref, sems, part, m, t).start()


def next_part(source_ref, target_ref, sems, part):
    for m in range(2):
        for t in range(2):
            fetch(source_ref, target_ref, sems, part, m, t).wait()
    start_fetch(source_ref, target_ref, sems, part + AHEAD)


def edge_kernel(source_ref, low_ref, high_ref, legendre_ref, sems):
    parts = sems.shape[0]
    chunk = source_ref.shape[2] // parts
    for part in range(AHEAD):
        start_fetch(source_ref, legendre_ref, sems, part)
    row = lax.broadcasted_iota(jnp.int32, (16, 256), 0)
    lane = lax.broadcasted_iota(jnp.int32, (16, 256), 1)
    cycle = (row & 1) + jnp.where(row >= 8, 126, 0)
    picks = []
    for m in range(2):
        pick = (((row >> 1) & 3) == 2 * m + (lane >> 7)) & ((lane & 127) == cycle)
        picks.append(pick.astype(F32).astype(BF16))
    for part in range(parts):
        place = slice(part * chunk, (part + 1) * chunk)
        edges = jnp.zeros((16, chunk), F32)
        next_part(source_ref, legendre_ref, sems, part)
        for m in range(2):
            table = jnp.concatenate([legendre_ref[m, 0, place], legendre_ref[m, 1, place]], axis=1)
            edges = edges + lax.dot_general(
                picks[m], table, (((1,), (1,)), ((), ())), preferred_element_type=F32
            )
        high_ref[:, place] = edges[0:8].astype(BF16)
        low_ref[:, place] = edges[8:16].astype(BF16)


def synth_kernel(
    m_ref, side_ref, beam_ref, spectra_ref, legendre_ref, own_ref, coef_ref, sums_ref
):
    rows, coef = scaled_rows(side_ref, beam_ref)
    square = rows * rows
    spectra = spectra_ref[...]
    pair = jnp.concatenate([spectra[0:1]] * 2 + [spectra[1:2]] * 2, axis=0)
    prior = square * jnp.concatenate([pair, pair], axis=0)
    norm_sum = square[:, 0:128]
    prior_sum = prior[:, 0:128]
    for start in range(128, rows.shape[1], 128):
        norm_sum = norm_sum + square[:, start : start + 128]
        prior_sum = prior_sum + prior[:, start : start + 128]
    sums_ref[...] = jnp.concatenate([norm_sum, prior_sum], axis=0) * 0.125
    own = []
    for m in range(2):
        table = jnp.concatenate([legendre_ref[m, 0], legendre_ref[m, 1]], axis=1)
        own.append(jnp.dot(coef, table, preferred_element_type=F32)[4 * m : 4 * m + 4])
    modes = jnp.concatenate(own, axis=0)
    fields = pltpu.roll(swap_rows(modes[:, 128:256]) - modes[:, 0:128], 2, 1)
    row = lax.broadcasted_iota(jnp.int32, (8, 128), 0)
    lane = lax.broadcasted_iota(jnp.int32, (8, 128), 1)
    own_ref[0:8] = jnp.where(lane < 2, 0.0, fields)
    mode = jnp.where(row < 4, m_ref[:, 0:1], m_ref[:, 1:2])
    high = jnp.where(lane < 2, fields, 0.0)
    high = jnp.where(lane == 4, (mode >> 6).astype(F32), high)
    own_ref[8:16] = jnp.where(lane == 5, (mode & 63).astype(F32), high)
    coef_ref[...] = coef


def both_modes(value, q):
    return jnp.concatenate([value[q : q + 1], value[q + 4 : q + 5]], axis=0)


def fields_kernel(coef_ref, low_ref, high_ref, own_ref, out_ref):
    rims = jnp.concatenate([low_ref[...], high_ref[...]], axis=0)
    rim = lax.dot_general(
        coef_ref[...], rims, (((1,), (1,)), ((), ())), preferred_element_type=F32
    )
    rim = jnp.concatenate([rim, jnp.zeros((8, 112), F32)], axis=1)
    row = lax.broadcasted_iota(jnp.int32, (8, 128), 0)
    lane = lax.broadcasted_iota(jnp.int32, (8, 128), 1)
    rim = jnp.where(row < 4, rim, pltpu.roll(rim, 124, 1))
    rim = swap_rows(pltpu.roll(rim, 126, 1)) - rim
    low = jnp.where(lane < 2, rim, own_ref[0:8])
    high = jnp.where((lane == 2) | (lane == 3), pltpu.roll(rim, 122, 1), own_ref[8:16])
    sent = to_pieces([both_modes(low, q) for q in range(4)], [both_modes(high, q) for q in range(4)], both_modes(high, 0), 4, 2)
    sent = sent.astype(BF16)
    for target in range(32):
        out_ref[target] = sent


def analysis_kernel(got_ref, low_ref, high_ref, legendre_ref, out_ref):
    total = got_ref[0].astype(F32)
    for source in range(1, 32):
        total = total + got_ref[source].astype(F32)
    lane = lax.broadcasted_iota(jnp.int32, (8, 128), 1)
    row = lax.broadcasted_iota(jnp.int32, (8, 128), 0)
    rest = total[:, 512:640]
    low = jnp.concatenate(
        [total[m : m + 1, 128 * q : 128 * q + 128] for m in range(2) for q in range(4)], axis=0
    )
    moved = [pltpu.roll(rest, 128 - 4 * q, 1) if q else rest for q in range(4)]
    high = jnp.concatenate([moved[q][m : m + 1] for m in range(2) for q in range(4)], axis=0)
    extra = jnp.broadcast_to(rest[0:1], (8, 128))
    curvature = jnp.sum(
        jnp.where((lane >= 16) & (lane < 19), extra, 0.0), axis=1, keepdims=True
    )
    norm = jnp.sum(jnp.where((lane >= 19) & (lane < 22), extra, 0.0), axis=1, keepdims=True)
    sums = jnp.zeros((8, 128), F32)
    for offset, piece in enumerate(split3(curvature) + split3(norm)):
        sums = jnp.where(lane == offset, piece, sums)
    sums = sums.astype(BF16)
    own = jnp.where(lane < 126, pltpu.roll(low, 126, 1), pltpu.roll(high, 126, 1))
    own_both = jnp.concatenate([-own, swap_rows(own)], axis=1)
    row_both = lax.broadcasted_iota(jnp.int32, (8, 256), 0)
    owns = []
    for m in range(2):
        owns.append(jnp.where((row_both >> 2) == m, own_both, 0.0).astype(BF16))
    low_swap, high_swap = swap_rows(low), swap_rows(high)
    rim = jnp.where(lane < 2, -low, jnp.where(lane < 4, pltpu.roll(low_swap, 2, 1), 0.0))
    rim = jnp.where((lane >= 8) & (lane < 10), pltpu.roll(-high, 6, 1), rim)
    rim = jnp.where((lane >= 10) & (lane < 12), pltpu.roll(high_swap, 8, 1), rim)
    rim = jnp.where(row < 4, rim, pltpu.roll(rim, 4, 1)).astype(BF16)


    bands = out_ref.shape[0]
    chunk = legendre_ref.shape[2] // bands
    for band in range(bands):
        place = slice(band * chunk, (band + 1) * chunk)
        rims = jnp.concatenate([low_ref[:, place], high_ref[:, place]], axis=0)
        result = jnp.dot(rim[:, 0:16], rims, preferred_element_type=F32)
        for m in range(2):
            table = jnp.concatenate([legendre_ref[m, 0, place], legendre_ref[m, 1, place]], axis=1)
            result = result + lax.dot_general(
                owns[m], table, (((1,), (1,)), ((), ())), preferred_element_type=F32
            )
        out_ref[band, :, 0:chunk] = result.astype(BF16)
        out_ref[band, :, chunk : chunk + 128] = sums


def update_kernel(parts_ref, share_ref, solution_ref, residual_ref):
    total = parts_ref[0].astype(F32)
    for source in range(1, parts_ref.shape[0]):
        total = total + parts_ref[source].astype(F32)
    length = share_ref.shape[1]
    rest = total[0:1, length : length + 128]
    lane = lax.broadcasted_iota(jnp.int32, (1, 128), 1)
    curvature = jnp.sum(jnp.where(lane < 3, rest, 0.0), axis=1, keepdims=True)
    norm = jnp.sum(jnp.where((lane >= 3) & (lane < 6), rest, 0.0), axis=1, keepdims=True)
    step = norm / curvature
    beam = share_ref[8:9]
    spectra = share_ref[9:11]
    pair = jnp.concatenate([spectra[0:1]] * 2 + [spectra[1:2]] * 2, axis=0)
    for m in range(2):
        side = share_ref[4 * m : 4 * m + 4]
        image = pair * side + beam * total[4 * m : 4 * m + 4, 0:length]
        solution_ref[m] = step * side
        residual_ref[m] = side - step * image


def local(
    right_side,
    inv_spectra,
    beam,
    m_values,
    legendre,
    stencil_weights,
    stencil_base,
    inv_noise,
    slot_counts,
):
    band_count = lax.axis_size("band")
    lmax_len = right_side.shape[2]
    share_len = lmax_len // band_count
    smem = pl.BlockSpec(memory_space=pltpu.SMEM)
    vmem = pl.BlockSpec(memory_space=pltpu.VMEM)
    params = pltpu.CompilerParams(vmem_limit_bytes=VMEM_LIMIT)
    stream_params = pltpu.CompilerParams(vmem_limit_bytes=STREAM_LIMIT)
    hbm = pl.BlockSpec(memory_space=pl.ANY)
    beam_row = beam.reshape(1, lmax_len)

    low_edge, high_edge, near_table = pl.pallas_call(
        edge_kernel,
        out_shape=(
            jax.ShapeDtypeStruct((8, lmax_len), BF16),
            jax.ShapeDtypeStruct((8, lmax_len), BF16),
            jax.ShapeDtypeStruct(legendre.shape, BF16),
        ),
        in_specs=[hbm],
        out_specs=(vmem, vmem, vmem),
        scratch_shapes=[pltpu.SemaphoreType.DMA((PARTS, 2, 2))],
        compiler_params=stream_params,
        name="edges",
    )(legendre)
    own_fields, coef, sums = pl.pallas_call(
        synth_kernel,
        out_shape=(
            jax.ShapeDtypeStruct((16, 128), F32),
            jax.ShapeDtypeStruct((8, lmax_len), BF16),
            jax.ShapeDtypeStruct((16, 128), F32),
        ),
        in_specs=[vmem] * 5,
        out_specs=(vmem, vmem, vmem),
        compiler_params=params,
        cost_estimate=pl.CostEstimate(flops=10**7, bytes_accessed=6 * 10**6, transcendentals=0),
        name="synth",
    )(m_values.reshape(1, 2), right_side, beam_row, inv_spectra, near_table)
    up = [(i, i + 1) for i in range(band_count - 1)]
    down = [(i + 1, i) for i in range(band_count - 1)]
    low_rim = lax.ppermute(low_edge, "band", up)
    high_rim = lax.ppermute(high_edge, "band", down)

    band = lax.axis_index("band").astype(jnp.int32).reshape(1)
    data, blocks, share = pl.pallas_call(
        pack_kernel,
        out_shape=(
            jax.ShapeDtypeStruct((24, 4096 + 128 + 3 * BLOCK), F32),
            jax.ShapeDtypeStruct((8, 128), jnp.int32),
            jax.ShapeDtypeStruct((16, share_len), F32),
        ),
        in_specs=[smem, smem] + [vmem] * 6,
        out_specs=(vmem, vmem, vmem),
        compiler_params=params,
        cost_estimate=pl.CostEstimate(flops=10**6, bytes_accessed=3 * 10**6, transcendentals=0),
        name="pack",
    )(
        band,
        slot_counts,
        stencil_weights.reshape(16, 32, 128),
        stencil_base.reshape(2, 32, 128),
        inv_noise.reshape(2, 32, 128),
        right_side,
        beam_row,
        inv_spectra,
    )

    sent = pl.pallas_call(
        fields_kernel,
        out_shape=jax.ShapeDtypeStruct((32, 2, PIECE), BF16),
        in_specs=[vmem, vmem, vmem, vmem],
        out_specs=vmem,
        compiler_params=params,
        name="fields",
    )(coef, low_rim, high_rim, own_fields)
    got = lax.all_to_all(sent, "harm", split_axis=0, concat_axis=0, tiled=True)

    back, table = pl.pallas_call(
        points_kernel,
        out_shape=(
            jax.ShapeDtypeStruct((32, 2, PIECE), BF16),
            jax.ShapeDtypeStruct(legendre.shape, BF16),
        ),
        in_specs=[vmem, vmem, vmem, vmem, hbm],
        out_specs=(vmem, vmem),
        scratch_shapes=[
            pltpu.VMEM((896, 256), BF16),
            pltpu.VMEM((256, LANES), BF16),
            pltpu.VMEM((256, LANES), F32),
            pltpu.VMEM((2, BLOCK), F32),
            pltpu.VMEM((ROWS, BLOCK), BF16),
            pltpu.VMEM((8, 64, BLOCK), F32),
            pltpu.VMEM((256, 4 * BLOCK), BF16),
            pltpu.VMEM((ROWS, 4 * BLOCK), BF16),
            pltpu.SemaphoreType.DMA(()),
        ],
        compiler_params=stream_params,
        name="points",
    )(blocks, sums, got, data, legendre)
    back_got = lax.all_to_all(back, "harm", split_axis=0, concat_axis=0, tiled=True)

    harmonic = pl.pallas_call(
        analysis_kernel,
        out_shape=jax.ShapeDtypeStruct((band_count, 8, share_len + 128), BF16),
        in_specs=[vmem, vmem, vmem, vmem],
        out_specs=vmem,
        compiler_params=params,
        name="analysis",
    )(back_got, low_rim, high_rim, table)
    parts = lax.all_to_all(harmonic, "band", split_axis=0, concat_axis=0, tiled=True)

    return pl.pallas_call(
        update_kernel,
        out_shape=(
            jax.ShapeDtypeStruct((2, 4, share_len), F32),
            jax.ShapeDtypeStruct((2, 4, share_len), F32),
        ),
        in_specs=[vmem, vmem],
        out_specs=(vmem, vmem),
        compiler_params=params,
        name="update",
    )(parts, share)


def solution(mesh):
    placed = (
        P("harm", None, None),
        P(),
        P(),
        P("harm"),
        P("harm", None, None, "band"),
        P(None, "harm", "band", None, None),
        P(None, "harm", "band", None, None),
        P(None, "harm", "band", None, None),
        P("harm", "band", None),
    )
    return jax.shard_map(
        local,
        mesh=mesh,
        in_specs=placed,
        out_specs=(P("harm", None, "band"), P("harm", None, "band")),
        check_vma=False,
    )
```

```python
import functools
import math

import jax
import jax.numpy as jnp
from jax import lax
from jax.experimental import pallas as pl
from jax.experimental.pallas import tpu as pltpu
from jax.sharding import PartitionSpec as P

NPHI = 20480
ROWS = 144
LANES = 256
PIECE = 640
BLOCK = 256
VMEM_LIMIT = 16 * 1024 * 1024
AHEAD = 4
PARTS = 2
STREAM_LIMIT = 46 * 1024 * 1024
F32 = jnp.float32
BF16 = jnp.bfloat16


def split3(value):
    first = value.astype(BF16).astype(F32)
    rest = value - first
    second = rest.astype(BF16).astype(F32)
    third = (rest - second).astype(BF16).astype(F32)
    return first, second, third


def trig_tables(modes):
    lane = lax.broadcasted_iota(jnp.int32, (64, 128), 1)
    digit = lane & 31
    steps = jnp.where(
        lane < 32, digit * 1024, jnp.where(lane < 64, digit * 32, jnp.where(lane < 96, digit, lane & 3))
    )
    product = modes * steps
    high = product >> 12
    turn = (high - 5 * ((high * 52429) >> 18)) * 4096 + (product & 4095)
    quarter = jnp.zeros_like(turn)
    for edge in (2560, 7680, 12800, 17920):
        quarter = quarter + (turn >= edge).astype(jnp.int32)
    angle = (turn - 5120 * quarter).astype(F32) * (2.0 * math.pi / NPHI)
    quarter = quarter & 3
    sq = angle * angle
    sine = angle * (1.0 + sq * (-1.0 / 6 + sq * (1.0 / 120 + sq * (-1.0 / 5040 + sq * (1.0 / 362880)))))
    cosine = 1.0 + sq * (
        -0.5 + sq * (1.0 / 24 + sq * (-1.0 / 720 + sq * (1.0 / 40320 - sq * (1.0 / 3628800))))
    )
    cos_out = jnp.where(
        quarter == 0, cosine, jnp.where(quarter == 1, -sine, jnp.where(quarter == 2, -cosine, sine))
    )
    sin_out = jnp.where(
        quarter == 0, sine, jnp.where(quarter == 1, cosine, jnp.where(quarter == 2, -sine, -cosine))
    )
    return cos_out, sin_out


def pack_kernel(
    band_ref, counts_ref, weights_ref, base_ref, noise_ref, side_ref, beam_ref, spectra_ref,
    data_ref, blocks_ref, share_ref,
):
    data_ref[...] = jnp.zeros_like(data_ref)
    lane = lax.broadcasted_iota(jnp.int32, (24, 128), 1)
    used = jnp.int32(0)
    for owner in range(32):
        count = counts_ref[0, 0, owner]
        pixel = base_ref[1, owner : owner + 1, :] + (owner * 640 - 2)
        if owner == 0:
            pixel = jnp.where(pixel < 0, pixel + NPHI, pixel)
        if owner == 31:
            pixel = jnp.where(pixel >= NPHI, pixel - NPHI, pixel)
        live = jnp.concatenate(
            [
                weights_ref[:, owner, :],
                base_ref[0, owner : owner + 1, :].astype(F32),
                pixel.astype(F32),
                noise_ref[:, owner, :],
                jnp.zeros((4, 128), F32),
            ],
            axis=0,
        )
        live = jnp.where(lane < count, live, 0.0)
        shift = used & 127
        live = pltpu.roll(live, shift, 1)
        start = pl.multiple_of((used >> 7) * 128, 128)
        here = data_ref[:, pl.ds(start, 128)]
        data_ref[:, pl.ds(start, 128)] = jnp.where(lane >= shift, live, here)
        after = pl.multiple_of(start + 128, 128)
        data_ref[:, pl.ds(after, 128)] = jnp.where(lane < shift, live, 0.0)
        used = used + count
    blocks_ref[...] = jnp.full(blocks_ref.shape, (used + (BLOCK - 1)) // BLOCK, jnp.int32)
    length = share_ref.shape[1]
    place = pl.ds(pl.multiple_of(band_ref[0] * length, 128), length)
    share_ref[0:4] = side_ref[0, :, place]
    share_ref[4:8] = side_ref[1, :, place]
    share_ref[8:9] = beam_ref[:, place]
    share_ref[9:11] = spectra_ref[:, place]
    share_ref[11:16] = jnp.zeros((5, length), F32)


def to_pieces(low, high, extra, first, count):
    lane = lax.broadcasted_iota(jnp.int32, low[0].shape, 1)
    rest = jnp.where((lane >= 16) & (lane < 16 + count), pltpu.roll(extra, 16 - first, 1), 0.0)
    for q in range(4):
        moved = pltpu.roll(high[q], 4 * q, 1) if q else high[q]
        rest = jnp.where((lane >= 4 * q) & (lane < 4 * q + 4), moved, rest)
    return jnp.concatenate(low + [rest], axis=1)


def points_kernel(
    blocks_ref, sums_ref, x_ref, data_ref, source_ref, out_ref, legendre_ref, table_ref, field_ref, acc_ref, curv_ref, grid_ref, wave_ref, term_ref, hit_ref, sem
):
    move = pltpu.make_async_copy(source_ref, legendre_ref, sem)
    move.start()
    got = jnp.concatenate([x_ref[source].astype(F32) for source in range(32)], axis=0)
    rest = got[:, 512:640]
    lane = lax.broadcasted_iota(jnp.int32, (64, 128), 1)
    for q in range(4):
        rows = slice(64 * q, 64 * q + 64)
        field_ref[rows, 0:128] = got[:, 128 * q : 128 * q + 128].astype(BF16)
        moved = pltpu.roll(rest, 128 - 4 * q, 1) if q else rest
        field_ref[rows, 128:256] = jnp.where(lane < 4, moved, 0.0).astype(BF16)
    grid_ref[...] = lax.broadcasted_iota(jnp.int32, (ROWS, BLOCK), 0).astype(F32).astype(BF16)
    mode_value = jnp.sum(
        jnp.where(lane == 16, rest * 64.0, jnp.where(lane == 17, rest, 0.0)), axis=1, keepdims=True
    )
    modes = jnp.broadcast_to(mode_value, (64, 128)).astype(jnp.int32)
    cos_tab, sin_tab = trig_tables(modes)
    weight = jnp.where(modes == 0, 1.0, 2.0).astype(F32) * 128.0**-0.5
    groups = [
        (lane < 32, weight),
        ((lane >= 32) & (lane < 64), None),
        ((lane >= 64) & (lane < 96), None),
    ]
    for a in range(4):
        groups.append(((lane >= 96) & (((lane - 96) & 15) >> 2 == a), None))
    for index, (mask, gain) in enumerate(groups):
        for part, table in enumerate((cos_tab, -sin_tab)):
            value = table if gain is None else table * gain
            value = jnp.where(mask, value, 0.0)
            rounded = value.astype(BF16)
            start = (2 * index + part) * 64
            table_ref[pl.ds(start, 64), 0:128] = rounded
            table_ref[pl.ds(start, 64), 128:256] = (value - rounded.astype(F32)).astype(BF16)
    acc_ref[...] = jnp.zeros_like(acc_ref)
    curv_ref[...] = jnp.zeros_like(curv_ref)
    one = jnp.ones((), BF16)
    zero = jnp.zeros((), BF16)

    term_ref[...] = jnp.zeros_like(term_ref)
    hit_ref[...] = jnp.zeros_like(hit_ref)

    def spread(slot):
        acc_ref[:, 0:ROWS] += lax.dot_general(
            term_ref[slot], hit_ref[slot], (((1,), (1,)), ((), ())), preferred_element_type=F32
        )

    def sample(index, slot):
        start = pl.multiple_of(index * BLOCK, BLOCK)
        info = data_ref[16:24, pl.ds(start, BLOCK)]
        first_row = info[0:1]
        grid_row = grid_ref[...]
        total = [None, None]
        for a in range(4):
            row_hit = jnp.where(grid_row == (first_row + float(a)).astype(BF16), one, zero)
            hit_ref[slot, :, a * BLOCK : (a + 1) * BLOCK] = row_hit
            picked = jnp.dot(field_ref[:, 0:ROWS], row_hit, preferred_element_type=F32)
            wave_re = wave_ref[slot, 2 * a]
            wave_im = wave_ref[slot, 2 * a + 1]
            for f in range(2):
                term = (
                    picked[128 * f : 128 * f + 64] * wave_re
                    + picked[128 * f + 64 : 128 * f + 128] * wave_im
                )
                total[f] = term if a == 0 else total[f] + term
        weighted = []
        for f in range(2):
            sampled = jnp.sum(total[f], axis=0, keepdims=True)
            value = info[2 + f : 3 + f] * sampled
            curv_ref[f : f + 1, :] += value * sampled
            weighted.append(value)
        for a in range(4):
            for f in range(2):
                for part in range(2):
                    row = 128 * f + 64 * part
                    term_ref[slot, row : row + 64, a * BLOCK : (a + 1) * BLOCK] = (
                        weighted[f] * wave_ref[slot, 2 * a + part]
                    ).astype(BF16)

    def turn(index, slot):
        data = data_ref[:, pl.ds(pl.multiple_of(index * BLOCK, BLOCK), BLOCK)]
        pixel = data[17:18].astype(jnp.int32)
        digit_id = grid_ref[0:32, :]
        hit = [
            jnp.where(digit_id == digit.astype(F32).astype(BF16), one, zero)
            for digit in (pixel >> 10, (pixel >> 5) & 31, pixel & 31)
        ]
        weights = data[0:16]
        weights_high = weights.astype(BF16)
        weights_low = (weights - weights_high.astype(F32)).astype(BF16)
        chosen = jnp.concatenate(hit + [weights_high, weights_low], axis=0)
        phases = jnp.dot(
            table_ref[...], jnp.concatenate([chosen, chosen], axis=0), preferred_element_type=F32
        )
        part = [phases[64 * i : 64 * (i + 1)] for i in range(14)]
        mid_re = part[0] * part[2] - part[1] * part[3]
        mid_im = part[0] * part[3] + part[1] * part[2]
        turn_re = mid_re * part[4] - mid_im * part[5]
        turn_im = mid_re * part[5] + mid_im * part[4]
        for a in range(4):
            wave_ref[slot, 2 * a] = turn_re * part[6 + 2 * a] - turn_im * part[7 + 2 * a]
            wave_ref[slot, 2 * a + 1] = turn_re * part[7 + 2 * a] + turn_im * part[6 + 2 * a]

    def pair_step(index, carry):
        turn(2 * index + 1, 1)
        sample(2 * index, 0)
        spread(1)
        turn(2 * index + 2, 0)
        sample(2 * index + 1, 1)
        spread(0)
        return carry

    count = jnp.max(blocks_ref[...])
    turn(0, 0)
    lax.fori_loop(0, count >> 1, pair_step, 0)
    spread(1)

    @pl.when((count & 1) == 1)
    def _():
        sample(count - 1, 0)
        spread(0)

    curvature = jnp.sum(curv_ref[...], axis=(0, 1), keepdims=True) + jnp.sum(
        sums_ref[8:16], axis=(0, 1), keepdims=True
    )
    norm = jnp.sum(sums_ref[0:8], axis=(0, 1), keepdims=True)
    extra = jnp.zeros((64, 128), F32)
    for offset, piece in enumerate(split3(curvature) + split3(norm)):
        extra = jnp.where(lane == offset, piece, extra)
    back = [acc_ref[64 * q : 64 * q + 64] for q in range(4)]
    sent = to_pieces([b[:, 0:128] for b in back], [b[:, 128:256] for b in back], extra, 0, 6)
    for target in range(32):
        out_ref[target] = sent[2 * target : 2 * target + 2].astype(BF16)
    move.wait()


def swap_rows(value):
    return jnp.concatenate(
        [
            value[3:4],
            -value[2:3],
            -value[1:2],
            value[0:1],
            value[7:8],
            -value[6:7],
            -value[5:6],
            value[4:5],
        ],
        axis=0,
    )


def scaled_rows(side_ref, beam_ref):
    rows = jnp.concatenate([side_ref[0], side_ref[1]], axis=0)
    return rows, (rows * beam_ref[...]).astype(BF16)


def fetch(source_ref, target_ref, sems, part, m, t):
    chunk = source_ref.shape[2] // sems.shape[0]
    place = pl.ds(part * chunk, chunk)
    return pltpu.make_async_copy(
        source_ref.at[m, t, place], target_ref.at[m, t, place], sems.at[part, m, t]
    )


def start_fetch(source_ref, target_ref, sems, part):
    if part < sems.shape[0]:
        for m in range(2):
            for t in range(2):
                fetch(source_ref, target_ref, sems, part, m, t).start()


def next_part(source_ref, target_ref, sems, part):
    for m in range(2):
        for t in range(2):
            fetch(source_ref, target_ref, sems, part, m, t).wait()
    start_fetch(source_ref, target_ref, sems, part + AHEAD)


def edge_kernel(source_ref, low_ref, high_ref, legendre_ref, sems):
    parts = sems.shape[0]
    chunk = source_ref.shape[2] // parts
    for part in range(AHEAD):
        start_fetch(source_ref, legendre_ref, sems, part)
    row = lax.broadcasted_iota(jnp.int32, (16, 256), 0)
    lane = lax.broadcasted_iota(jnp.int32, (16, 256), 1)
    cycle = (row & 1) + jnp.where(row >= 8, 126, 0)
    picks = []
    for m in range(2):
        pick = (((row >> 1) & 3) == 2 * m + (lane >> 7)) & ((lane & 127) == cycle)
        picks.append(pick.astype(F32).astype(BF16))
    for part in range(parts):
        place = slice(part * chunk, (part + 1) * chunk)
        edges = jnp.zeros((16, chunk), F32)
        next_part(source_ref, legendre_ref, sems, part)
        for m in range(2):
            table = jnp.concatenate([legendre_ref[m, 0, place], legendre_ref[m, 1, place]], axis=1)
            edges = edges + lax.dot_general(
                picks[m], table, (((1,), (1,)), ((), ())), preferred_element_type=F32
            )
        high_ref[:, place] = edges[0:8].astype(BF16)
        low_ref[:, place] = edges[8:16].astype(BF16)


def synth_kernel(
    m_ref, side_ref, beam_ref, spectra_ref, legendre_ref, own_ref, coef_ref, sums_ref
):
    rows, coef = scaled_rows(side_ref, beam_ref)
    square = rows * rows
    spectra = spectra_ref[...]
    pair = jnp.concatenate([spectra[0:1]] * 2 + [spectra[1:2]] * 2, axis=0)
    prior = square * jnp.concatenate([pair, pair], axis=0)
    norm_sum = square[:, 0:128]
    prior_sum = prior[:, 0:128]
    for start in range(128, rows.shape[1], 128):
        norm_sum = norm_sum + square[:, start : start + 128]
        prior_sum = prior_sum + prior[:, start : start + 128]
    sums_ref[...] = jnp.concatenate([norm_sum, prior_sum], axis=0) * 0.125
    own = []
    for m in range(2):
        table = jnp.concatenate([legendre_ref[m, 0], legendre_ref[m, 1]], axis=1)
        own.append(jnp.dot(coef, table, preferred_element_type=F32)[4 * m : 4 * m + 4])
    modes = jnp.concatenate(own, axis=0)
    fields = pltpu.roll(swap_rows(modes[:, 128:256]) - modes[:, 0:128], 2, 1)
    row = lax.broadcasted_iota(jnp.int32, (8, 128), 0)
    lane = lax.broadcasted_iota(jnp.int32, (8, 128), 1)
    own_ref[0:8] = jnp.where(lane < 2, 0.0, fields)
    mode = jnp.where(row < 4, m_ref[:, 0:1], m_ref[:, 1:2])
    high = jnp.where(lane < 2, fields, 0.0)
    high = jnp.where(lane == 4, (mode >> 6).astype(F32), high)
    own_ref[8:16] = jnp.where(lane == 5, (mode & 63).astype(F32), high)
    coef_ref[...] = coef


def both_modes(value, q):
    return jnp.concatenate([value[q : q + 1], value[q + 4 : q + 5]], axis=0)


def fields_kernel(coef_ref, low_ref, high_ref, own_ref, out_ref):
    rims = jnp.concatenate([low_ref[...], high_ref[...]], axis=0)
    rim = lax.dot_general(
        coef_ref[...], rims, (((1,), (1,)), ((), ())), preferred_element_type=F32
    )
    rim = jnp.concatenate([rim, jnp.zeros((8, 112), F32)], axis=1)
    row = lax.broadcasted_iota(jnp.int32, (8, 128), 0)
    lane = lax.broadcasted_iota(jnp.int32, (8, 128), 1)
    rim = jnp.where(row < 4, rim, pltpu.roll(rim, 124, 1))
    rim = swap_rows(pltpu.roll(rim, 126, 1)) - rim
    low = jnp.where(lane < 2, rim, own_ref[0:8])
    high = jnp.where((lane == 2) | (lane == 3), pltpu.roll(rim, 122, 1), own_ref[8:16])
    sent = to_pieces([both_modes(low, q) for q in range(4)], [both_modes(high, q) for q in range(4)], both_modes(high, 0), 4, 2)
    sent = sent.astype(BF16)
    for target in range(32):
        out_ref[target] = sent


def both_halves(value):
    rounded = value.astype(BF16)
    return jnp.concatenate([rounded, (value - rounded.astype(F32)).astype(BF16)], axis=0)


def analysis_kernel(got_ref, low_ref, high_ref, legendre_ref, out_ref):
    total = got_ref[0].astype(F32)
    for source in range(1, 32):
        total = total + got_ref[source].astype(F32)
    lane = lax.broadcasted_iota(jnp.int32, (8, 128), 1)
    row = lax.broadcasted_iota(jnp.int32, (8, 128), 0)
    rest = total[:, 512:640]
    low = jnp.concatenate(
        [total[m : m + 1, 128 * q : 128 * q + 128] for m in range(2) for q in range(4)], axis=0
    )
    moved = [pltpu.roll(rest, 128 - 4 * q, 1) if q else rest for q in range(4)]
    high = jnp.concatenate([moved[q][m : m + 1] for m in range(2) for q in range(4)], axis=0)
    extra = jnp.broadcast_to(rest[0:1], (8, 128))
    curvature = jnp.sum(
        jnp.where((lane >= 16) & (lane < 19), extra, 0.0), axis=1, keepdims=True
    )
    norm = jnp.sum(jnp.where((lane >= 19) & (lane < 22), extra, 0.0), axis=1, keepdims=True)
    sums = jnp.zeros((8, 128), F32)
    for offset, piece in enumerate(split3(curvature) + split3(norm)):
        sums = jnp.where(lane == offset, piece, sums)
    sums = sums.astype(BF16)
    own = jnp.where(lane < 126, pltpu.roll(low, 126, 1), pltpu.roll(high, 126, 1))
    own_both = jnp.concatenate([-own, swap_rows(own)], axis=1)
    row_both = lax.broadcasted_iota(jnp.int32, (8, 256), 0)
    owns = []
    for m in range(2):
        owns.append(both_halves(jnp.where((row_both >> 2) == m, own_both, 0.0)))
    low_swap, high_swap = swap_rows(low), swap_rows(high)
    rim = jnp.where(lane < 2, -low, jnp.where(lane < 4, pltpu.roll(low_swap, 2, 1), 0.0))
    rim = jnp.where((lane >= 8) & (lane < 10), pltpu.roll(-high, 6, 1), rim)
    rim = jnp.where((lane >= 10) & (lane < 12), pltpu.roll(high_swap, 8, 1), rim)
    rim = both_halves(jnp.where(row < 4, rim, pltpu.roll(rim, 4, 1)))


    bands = out_ref.shape[0]
    chunk = legendre_ref.shape[2] // bands
    for band in range(bands):
        place = slice(band * chunk, (band + 1) * chunk)
        rims = jnp.concatenate([low_ref[:, place], high_ref[:, place]], axis=0)
        result = jnp.dot(rim[:, 0:16], rims, preferred_element_type=F32)
        for m in range(2):
            table = jnp.concatenate([legendre_ref[m, 0, place], legendre_ref[m, 1, place]], axis=1)
            result = result + lax.dot_general(
                owns[m], table, (((1,), (1,)), ((), ())), preferred_element_type=F32
            )
        out_ref[band, :, 0:chunk] = (result[0:8] + result[8:16]).astype(BF16)
        out_ref[band, :, chunk : chunk + 128] = sums


def update_kernel(parts_ref, share_ref, solution_ref, residual_ref):
    total = parts_ref[0].astype(F32)
    for source in range(1, parts_ref.shape[0]):
        total = total + parts_ref[source].astype(F32)
    length = share_ref.shape[1]
    rest = total[0:1, length : length + 128]
    lane = lax.broadcasted_iota(jnp.int32, (1, 128), 1)
    curvature = jnp.sum(jnp.where(lane < 3, rest, 0.0), axis=1, keepdims=True)
    norm = jnp.sum(jnp.where((lane >= 3) & (lane < 6), rest, 0.0), axis=1, keepdims=True)
    step = norm / curvature
    beam = share_ref[8:9]
    spectra = share_ref[9:11]
    pair = jnp.concatenate([spectra[0:1]] * 2 + [spectra[1:2]] * 2, axis=0)
    for m in range(2):
        side = share_ref[4 * m : 4 * m + 4]
        image = pair * side + beam * total[4 * m : 4 * m + 4, 0:length]
        solution_ref[m] = step * side
        residual_ref[m] = side - step * image


def local(
    right_side,
    inv_spectra,
    beam,
    m_values,
    legendre,
    stencil_weights,
    stencil_base,
    inv_noise,
    slot_counts,
):
    band_count = lax.axis_size("band")
    lmax_len = right_side.shape[2]
    share_len = lmax_len // band_count
    smem = pl.BlockSpec(memory_space=pltpu.SMEM)
    vmem = pl.BlockSpec(memory_space=pltpu.VMEM)
    params = pltpu.CompilerParams(vmem_limit_bytes=VMEM_LIMIT)
    stream_params = pltpu.CompilerParams(vmem_limit_bytes=STREAM_LIMIT)
    hbm = pl.BlockSpec(memory_space=pl.ANY)
    beam_row = beam.reshape(1, lmax_len)

    low_edge, high_edge, near_table = pl.pallas_call(
        edge_kernel,
        out_shape=(
            jax.ShapeDtypeStruct((8, lmax_len), BF16),
            jax.ShapeDtypeStruct((8, lmax_len), BF16),
            jax.ShapeDtypeStruct(legendre.shape, BF16),
        ),
        in_specs=[hbm],
        out_specs=(vmem, vmem, vmem),
        scratch_shapes=[pltpu.SemaphoreType.DMA((PARTS, 2, 2))],
        compiler_params=stream_params,
        name="edges",
    )(legendre)
    own_fields, coef, sums = pl.pallas_call(
        synth_kernel,
        out_shape=(
            jax.ShapeDtypeStruct((16, 128), F32),
            jax.ShapeDtypeStruct((8, lmax_len), BF16),
            jax.ShapeDtypeStruct((16, 128), F32),
        ),
        in_specs=[vmem] * 5,
        out_specs=(vmem, vmem, vmem),
        compiler_params=params,
        cost_estimate=pl.CostEstimate(flops=10**7, bytes_accessed=6 * 10**6, transcendentals=0),
        name="synth",
    )(m_values.reshape(1, 2), right_side, beam_row, inv_spectra, near_table)
    up = [(i, i + 1) for i in range(band_count - 1)]
    down = [(i + 1, i) for i in range(band_count - 1)]
    low_rim = lax.ppermute(low_edge, "band", up)
    high_rim = lax.ppermute(high_edge, "band", down)

    band = lax.axis_index("band").astype(jnp.int32).reshape(1)
    data, blocks, share = pl.pallas_call(
        pack_kernel,
        out_shape=(
            jax.ShapeDtypeStruct((24, 4096 + 128 + 3 * BLOCK), F32),
            jax.ShapeDtypeStruct((8, 128), jnp.int32),
            jax.ShapeDtypeStruct((16, share_len), F32),
        ),
        in_specs=[smem, smem] + [vmem] * 6,
        out_specs=(vmem, vmem, vmem),
        compiler_params=params,
        cost_estimate=pl.CostEstimate(flops=10**6, bytes_accessed=3 * 10**6, transcendentals=0),
        name="pack",
    )(
        band,
        slot_counts,
        stencil_weights.reshape(16, 32, 128),
        stencil_base.reshape(2, 32, 128),
        inv_noise.reshape(2, 32, 128),
        right_side,
        beam_row,
        inv_spectra,
    )

    sent = pl.pallas_call(
        fields_kernel,
        out_shape=jax.ShapeDtypeStruct((32, 2, PIECE), BF16),
        in_specs=[vmem, vmem, vmem, vmem],
        out_specs=vmem,
        compiler_params=params,
        name="fields",
    )(coef, low_rim, high_rim, own_fields)
    got = lax.all_to_all(sent, "harm", split_axis=0, concat_axis=0, tiled=True)

    back, table = pl.pallas_call(
        points_kernel,
        out_shape=(
            jax.ShapeDtypeStruct((32, 2, PIECE), BF16),
            jax.ShapeDtypeStruct(legendre.shape, BF16),
        ),
        in_specs=[vmem, vmem, vmem, vmem, hbm],
        out_specs=(vmem, vmem),
        scratch_shapes=[
            pltpu.VMEM((896, 256), BF16),
            pltpu.VMEM((256, LANES), BF16),
            pltpu.VMEM((256, LANES), F32),
            pltpu.VMEM((2, BLOCK), F32),
            pltpu.VMEM((ROWS, BLOCK), BF16),
            pltpu.VMEM((2, 8, 64, BLOCK), F32),
            pltpu.VMEM((2, 256, 4 * BLOCK), BF16),
            pltpu.VMEM((2, ROWS, 4 * BLOCK), BF16),
            pltpu.SemaphoreType.DMA(()),
        ],
        compiler_params=stream_params,
        name="points",
    )(blocks, sums, got, data, legendre)
    back_got = lax.all_to_all(back, "harm", split_axis=0, concat_axis=0, tiled=True)

    harmonic = pl.pallas_call(
        analysis_kernel,
        out_shape=jax.ShapeDtypeStruct((band_count, 8, share_len + 128), BF16),
        in_specs=[vmem, vmem, vmem, vmem],
        out_specs=vmem,
        compiler_params=params,
        name="analysis",
    )(back_got, low_rim, high_rim, table)
    parts = lax.all_to_all(harmonic, "band", split_axis=0, concat_axis=0, tiled=True)

    return pl.pallas_call(
        update_kernel,
        out_shape=(
            jax.ShapeDtypeStruct((2, 4, share_len), F32),
            jax.ShapeDtypeStruct((2, 4, share_len), F32),
        ),
        in_specs=[vmem, vmem],
        out_specs=(vmem, vmem),
        compiler_params=params,
        name="update",
    )(parts, share)


def solution(mesh):
    placed = (
        P("harm", None, None),
        P(),
        P(),
        P("harm"),
        P("harm", None, None, "band"),
        P(None, "harm", "band", None, None),
        P(None, "harm", "band", None, None),
        P(None, "harm", "band", None, None),
        P("harm", "band", None),
    )
    return jax.shard_map(
        local,
        mesh=mesh,
        in_specs=placed,
        out_specs=(P("harm", None, "band"), P("harm", None, "band")),
        check_vma=False,
    )
```
